512 devices in a mesh: agents: 64 (over y_lo, z, core), heads: 8 (over x, y_hi).
Axes of the slice: x: 4, y: 8 (y_hi: 2, y_lo: 4; y = y_hi * 4 + y_lo), z: 8, core: 2. Of those that a mesh axis runs over, the one named last changes fastest.
Arguments:
- queries: bfloat16 [128, 8192], P('agents', 'heads'), as said below
- global_kv: bfloat16 [2, 32768, 1024], P(None, 'agents', 'heads'), as said below
- team_kv: bfloat16 [2, 131072, 1024], P(None, 'agents', 'heads'), may hold values from -8 to 8
- suffix_kv: bfloat16 [2, 128, 128, 1024], P(None, 'agents', None, 'heads'), may hold values from -10 to 10
- team_lengths: int32 [64], replicated, may hold values from 128 to 2048, as said below
- team_map: int32 [128], replicated, may hold values from 0 to 63, as said below
- suffix_lengths: int32 [128], P('agents'), may hold values from 1 to 128, as said below
- team_owner: int32 [64], replicated, may hold values from 0 to 63, each once
- out_weight: bfloat16 [8192, 8192], P('heads', 'agents'), may hold values from -0.0625 to 0.0625
Outputs:
- layer_out: bfloat16 [128, 8192], P('heads', 'agents')
The draws below stay inside these ranges and needn't reach their ends.
Inputs may be any that keep to these rules, and one draw needn't show every extreme that they name: `queries`: entries of order one; a few agents may have much larger entries. `global_kv`: entries of order one. `team_lengths`: every team prompt has at most 2048 tokens and some team has exactly 2048. `team_map`: no team has more than 8 agents and some team has exactly 8. `suffix_lengths`: every suffix has at most 128 tokens and some agent has exactly 128. `team_owner`: each index of agents owns exactly one team.
All inputs are finite; a program needn't handle non-finite values.
Results may differ from the reference program's by a relative error of at most 0.017.
Values may be sent and summed in bfloat16 or wider, within the bound.
A program may use at most 192 MiB of HBM per device.

```python
import math
import jax
import jax.numpy as jnp
from jax import lax

D = 8192
QHEADS = 64
KVHEADS = 8
HEAD_DIM = 128
TEAM_MAX = 2048
SUF_MAX = 128
AGENTS = 128
GLOBAL = 32768
TEAMS = 64
TEAM_CAP = 8


def global_pattern(key):
    keys_base = jax.random.normal(jax.random.fold_in(key, 11), (GLOBAL, KVHEADS, HEAD_DIM), jnp.float32)
    return keys_base


def draw_global_kv(key, part):
    keys_base = global_pattern(key)
    scaled = keys_base
    values = jax.random.normal(jax.random.fold_in(key, 17), (GLOBAL, KVHEADS, HEAD_DIM), jnp.float32)
    stacked = jnp.stack([scaled, values]).reshape(2, GLOBAL, KVHEADS * HEAD_DIM)
    return stacked.astype(jnp.bfloat16)


def draw_queries(key, part):
    mixed = 2.0 * jax.random.normal(jax.random.fold_in(key, 22), (AGENTS, QHEADS, HEAD_DIM), jnp.float32)
    return mixed.reshape(AGENTS, QHEADS * HEAD_DIM).astype(jnp.bfloat16)


def draw_team_lengths(key, part):
    drawn = jax.random.randint(jax.random.fold_in(key, 31), (TEAMS,), TEAM_MAX // 16, TEAM_MAX + 1)
    chosen_one = jax.random.randint(jax.random.fold_in(key, 32), (), 0, TEAMS)
    return jnp.where(jnp.arange(TEAMS) == chosen_one, TEAM_MAX, drawn).astype(jnp.int32)


def draw_suffix_lengths(key, part):
    drawn = jax.random.randint(jax.random.fold_in(key, 33), (AGENTS,), 1, SUF_MAX + 1)
    chosen_one = jax.random.randint(jax.random.fold_in(key, 34), (), 0, AGENTS)
    return jnp.where(jnp.arange(AGENTS) == chosen_one, SUF_MAX, drawn).astype(jnp.int32)


def draw_team_map(key, part):
    ranking = jax.random.permutation(jax.random.fold_in(key, 41), TEAMS)
    others = TEAMS - 1
    slot_ids = jnp.arange(others * TEAM_CAP)
    slot_rank = slot_ids // TEAM_CAP + 1
    within = slot_ids % TEAM_CAP
    room = TEAM_CAP // (1 + slot_rank % 4)
    shuffled = jax.random.permutation(jax.random.fold_in(key, 42), others * TEAM_CAP)
    ordering = jnp.where(within < room, shuffled, shuffled + others * TEAM_CAP)
    taken = jnp.argsort(ordering)[:AGENTS - TEAM_CAP]
    listed = jnp.concatenate([jnp.full((TEAM_CAP,), ranking[0], jnp.int32), ranking[slot_rank[taken]].astype(jnp.int32)])
    spread = jax.random.permutation(jax.random.fold_in(key, 43), AGENTS)
    return listed[spread].astype(jnp.int32)


def steps_of(own_key, shape, cuts, least, high):
    factor_of = 1.0
    for position, shards_of in cuts:
        heights = jax.random.uniform(jax.random.fold_in(jax.random.fold_in(own_key, 6), position), (shards_of,), jnp.float32, least / len(cuts), high / len(cuts))
        factor_of = factor_of * jnp.repeat(jnp.exp(heights), shape[position] // shards_of).reshape((-1,) + (1,) * (len(shape) - 1 - position))
    return factor_of


def gaussian(own_key, shape, scale, limit, shards=(), held_as=jnp.bfloat16):
    values = scale * jax.random.normal(own_key, shape, jnp.float32)
    if shards:
        values = values * steps_of(own_key, shape, shards, -0.22, 0.18)
    return jnp.clip(values, -limit, limit).astype(held_as)


def setup_inputs(seed: int = 0) -> dict:
    key_list = jax.random.split(jax.random.key(seed), 10)
    queries = draw_queries(jax.random.fold_in(key_list[9], 71), 0)
    global_kv = draw_global_kv(jax.random.fold_in(key_list[9], 71), 0)
    team_kv = gaussian(key_list[2], (2, TEAMS * TEAM_MAX, KVHEADS * HEAD_DIM), 1.25, 8.0, ((1, 64), (2, 8)))
    suffix_kv = gaussian(key_list[3], (2, AGENTS, SUF_MAX, KVHEADS * HEAD_DIM), 1.75, 10.0, ((1, 64), (3, 8)))
    team_lengths = draw_team_lengths(jax.random.fold_in(key_list[9], 71), 0)
    team_map = draw_team_map(jax.random.fold_in(key_list[9], 71), 0)
    suffix_lengths = draw_suffix_lengths(jax.random.fold_in(key_list[9], 71), 0)
    team_owner = jax.random.permutation(key_list[7], TEAMS).astype(jnp.int32)
    out_weight = gaussian(key_list[8], (QHEADS * HEAD_DIM, D), (QHEADS * HEAD_DIM) ** -0.5, 0.0625, ((0, 8), (1, 64)))
    return dict(queries=queries, global_kv=global_kv, team_kv=team_kv, suffix_kv=suffix_kv, team_lengths=team_lengths, team_map=team_map, suffix_lengths=suffix_lengths, team_owner=team_owner, out_weight=out_weight)


NEG = -1e+30

def round_weights(weights):
    rounded = lax.optimization_barrier(weights.astype(jnp.bfloat16))
    return rounded.astype(jnp.float32)

def reference(queries, global_kv, team_kv, suffix_kv, team_lengths, team_map, suffix_lengths, team_owner, out_weight):
    highest_precision = lax.Precision.HIGHEST
    group_size = QHEADS // KVHEADS
    scaling = 1.0 / math.sqrt(HEAD_DIM)
    glob_keys = global_kv[0].reshape(GLOBAL, KVHEADS, HEAD_DIM).astype(jnp.float32)
    glob_values = global_kv[1].reshape(GLOBAL, KVHEADS, HEAD_DIM).astype(jnp.float32)
    team_keys = team_kv[0].reshape(TEAMS, TEAM_MAX, KVHEADS, HEAD_DIM)
    team_values = team_kv[1].reshape(TEAMS, TEAM_MAX, KVHEADS, HEAD_DIM)
    batch_size = math.gcd(AGENTS, 8)
    batches = AGENTS // batch_size
    query_blocks = queries.reshape(batches, batch_size, KVHEADS, group_size, HEAD_DIM)
    team_blocks = team_map.reshape(batches, batch_size)
    suffix_blocks = suffix_kv.reshape(2, batches, batch_size, SUF_MAX, KVHEADS, HEAD_DIM).transpose(1, 0, 2, 3, 4, 5)
    suffix_len_blocks = suffix_lengths.reshape(batches, batch_size)

    def attend(items):
        query_block, team_block, suffix_block, suffix_len = items
        query_float = query_block.astype(jnp.float32)
        slab_ids = team_owner[team_block]
        block_team_keys = team_keys[slab_ids].astype(jnp.float32)
        block_team_values = team_values[slab_ids].astype(jnp.float32)
        glob_scores = jnp.einsum('ajgd,tjd->ajgt', query_float, glob_keys, precision=highest_precision) * scaling
        team_scores = jnp.einsum('ajgd,asjd->ajgs', query_float, block_team_keys, precision=highest_precision) * scaling
        suffix_scores = jnp.einsum('ajgd,asjd->ajgs', query_float, suffix_block[0].astype(jnp.float32), precision=highest_precision) * scaling
        team_ok = (jnp.arange(TEAM_MAX, dtype=jnp.int32)[None, :] < team_lengths[team_block][:, None])[:, None, None, :]
        suffix_ok = (jnp.arange(SUF_MAX, dtype=jnp.int32)[None, :] < suffix_len[:, None])[:, None, None, :]
        team_scores = jnp.where(team_ok, team_scores, NEG)
        suffix_scores = jnp.where(suffix_ok, suffix_scores, NEG)
        overall = jnp.maximum(lax.optimization_barrier(jnp.max(glob_scores, axis=-1)), jnp.maximum(lax.optimization_barrier(jnp.max(team_scores, axis=-1)), lax.optimization_barrier(jnp.max(suffix_scores, axis=-1))))
        overall = overall[..., None]
        glob_weights = jnp.exp(glob_scores - overall)
        team_weights = jnp.where(team_ok, jnp.exp(team_scores - overall), 0.0)
        suffix_weights = jnp.where(suffix_ok, jnp.exp(suffix_scores - overall), 0.0)
        total_weight = lax.optimization_barrier(jnp.sum(glob_weights, axis=-1)) + lax.optimization_barrier(jnp.sum(team_weights, axis=-1)) + lax.optimization_barrier(jnp.sum(suffix_weights, axis=-1))
        numerator = jnp.einsum('ajgt,tjd->ajgd', round_weights(glob_weights), glob_values, precision=highest_precision)
        numerator = numerator + jnp.einsum('ajgs,asjd->ajgd', round_weights(team_weights), block_team_values, precision=highest_precision)
        numerator = numerator + jnp.einsum('ajgs,asjd->ajgd', round_weights(suffix_weights), suffix_block[1].astype(jnp.float32), precision=highest_precision)
        return (numerator / total_weight[..., None]).reshape(batch_size, QHEADS * HEAD_DIM)
    attention = lax.map(attend, (query_blocks, team_blocks, suffix_blocks, suffix_len_blocks))
    attention = attention.reshape(AGENTS, QHEADS * HEAD_DIM).astype(jnp.bfloat16)
    return jnp.dot(attention, out_weight, preferred_element_type=jnp.float32).astype(jnp.bfloat16)
```

```python
import math

import jax
import jax.numpy as jnp
from jax import lax
from jax.experimental import pallas as pl
from jax.experimental.pallas import tpu as pltpu
from jax.sharding import PartitionSpec as P

HEAD_DIM = 128
TEAM_CAP = 8
NEG = -1e30
MESH = pl.DeviceIdType.MESH
F32 = jnp.float32
BF16 = jnp.bfloat16


def dot(a, b):
    return jnp.dot(a, b, preferred_element_type=F32)


def dot_t(a, b):
    return lax.dot_general(a, b, (((1,), (1,)), ((), ())), preferred_element_type=F32)


def iota(shape, dim):
    return lax.broadcasted_iota(jnp.int32, shape, dim)


def softmax_part(scores, values, scaling):
    high = jnp.max(scores, axis=-1, keepdims=True)
    weights = jnp.exp((scores - high) * scaling)
    mass = jnp.sum(weights, axis=-1, keepdims=True)
    return dot(weights.astype(BF16), values), high, mass


def make_kernel(agent_devices, head_devices):
    chips = agent_devices // 2
    rows = chips * 16

    def kernel(
        q_ref, lengths_ref, map_ref, owner_ref, suffix_len_ref,
        global_hbm, team_hbm, suffix_hbm, weight_hbm,
        out_ref,
        q_f32, q_own, q_all, global_kv, team_kv, suffix_kv, weight,
        part_out, part_in, lse_out, lse_in, att_own, att_all, att_f32,
        proj_out, proj_in, merged,
        local_sem, send_sem, recv_sem,
    ):
        a = lax.axis_index("agents")
        h = lax.axis_index("heads")
        core = lax.rem(a, 2)
        chip = a // 2
        scaling = 1.0 / math.sqrt(HEAD_DIM)

        def same_core(k):
            return (lax.rem(chip + k, chips) * 2 + core, h)

        def head_peer(k, d):
            return (chip * 2 + lax.rem(core + d, 2), lax.rem(h + k, head_devices))

        sibling = head_peer(0, 1)
        peers = [same_core(k) for k in range(1, chips)]
        heads = [(k, d) for k in range(head_devices) for d in range(2) if k or d]

        barrier = pltpu.get_barrier_semaphore()
        for peer in peers + [head_peer(k, d) for k, d in heads]:
            pl.semaphore_signal(barrier, inc=1, device_id=peer, device_id_type=MESH)

        span = global_hbm.shape[1]
        own_span = pl.ds(pl.multiple_of(core * span, span), span)
        local = [
            pltpu.make_async_copy(global_hbm, global_kv.at[:, own_span], local_sem.at[0]),
            pltpu.make_async_copy(team_hbm, team_kv.at[core], local_sem.at[1]),
            pltpu.make_async_copy(suffix_hbm, suffix_kv, local_sem.at[2]),
            pltpu.make_async_copy(weight_hbm, weight.at[core], local_sem.at[3]),
        ]
        for copy in local:
            copy.start()

        for i in range(2):
            for j in range(8):
                q_f32[pl.ds(i * 8 + j, 1), :] = q_ref[
                    pl.ds(i, 1), pl.ds(j * HEAD_DIM, HEAD_DIM)
                ].astype(F32)
        q_own[...] = q_f32[...].astype(BF16)

        pl.semaphore_wait(barrier, len(peers) + len(heads))

        own_rows = pl.ds(pl.multiple_of(chip * 16, 16), 16)

        def send(src, dst, s, peer):
            copy = pltpu.make_async_remote_copy(
                src_ref=src, dst_ref=dst, send_sem=send_sem.at[s], recv_sem=recv_sem.at[s],
                device_id=peer, device_id_type=MESH,
            )
            copy.start()

        def keep(src, dst, s):
            pltpu.make_async_copy(src, dst, recv_sem.at[s]).start()

        def arrived(ref, s):
            pltpu.make_async_copy(ref, ref, recv_sem.at[s]).wait()

        def sent(ref, s):
            pltpu.make_async_copy(ref, ref, send_sem.at[s]).wait()

        for peer in peers:
            send(q_own, q_all.at[own_rows], 0, peer)
        keep(q_own, q_all.at[own_rows], 0)
        send(global_hbm, global_kv.at[:, own_span], 1, sibling)
        send(team_hbm, team_kv.at[core], 2, sibling)
        send(weight_hbm, weight.at[core], 3, sibling)

        agents = map_ref.shape[1]
        team_of = map_ref[...]
        agent = iota((1, agents), 1)
        mine = lax.rem(agent // 2, 2) == core
        before = (iota((agents, agents), 0) < iota((agents, agents), 1)).astype(BF16)
        row_agent = iota((agents, rows), 1)
        row_agent = (row_agent // 16) * 4 + core * 2 + (row_agent // 8) % 2
        spread = (iota((agents, rows), 0) == row_agent).astype(BF16)
        owner = owner_ref[...]
        team_ids = iota(owner.shape, 1)
        picks, spans = [], []
        for slot in range(2):
            here = owner == chip * 2 + slot
            team = jnp.sum(jnp.where(here, team_ids, 0), axis=1, keepdims=True)
            spans.append(jnp.sum(jnp.where(here, lengths_ref[...], 0), axis=1, keepdims=True))
            member = jnp.logical_and(team_of == team, mine)
            members = jnp.broadcast_to(jnp.where(member, 1.0, 0.0), (8, agents)).astype(BF16)
            rank = dot(members, before)[0:1]
            code = jnp.where(member, rank, 255.0)
            picks.append(dot(jnp.broadcast_to(code, (8, agents)).astype(BF16), spread)[0:1])
        place = iota((TEAM_CAP * 8, rows), 0)
        same_head = place % 8 == iota((TEAM_CAP * 8, rows), 1) % 8
        take = jnp.concatenate(
            [
                jnp.where(
                    jnp.logical_and(code == (place // 8).astype(F32), same_head), 1.0, 0.0
                )
                for code in picks
            ],
            axis=0,
        )
        give = take.T
        take = take.astype(BF16)

        local[2].wait()
        suffix_num, suffix_lse = [], []
        for i in range(2):
            scores = dot_t(q_own[...], suffix_kv[0, i])[i * 8 : i * 8 + 8]
            seen = iota(scores.shape, 1) < suffix_len_ref[i]
            high = jnp.max(jnp.where(seen, scores, NEG), axis=-1, keepdims=True)
            weights = jnp.where(seen, jnp.exp((jnp.minimum(scores, high) - high) * scaling), 0.0)
            mass = jnp.sum(weights, axis=-1, keepdims=True)
            weights = jnp.concatenate([weights, weights], axis=0).astype(BF16)
            num = dot(weights, suffix_kv[1, i])[0:8]
            suffix_num.append(num / mass)
            suffix_lse.append(high * scaling + jnp.log(mass))
        suffix_num = jnp.concatenate(suffix_num, axis=0)
        suffix_lse = jnp.concatenate(suffix_lse, axis=0)

        local[0].wait()
        local[1].wait()
        arrived(global_hbm, 1)
        arrived(team_hbm, 2)
        arrived(q_all, 0)

        team_rows = dot(take, q_all[...]).astype(BF16)
        team_num, team_high, team_mass = [], [], []
        for slot in range(2):
            block = TEAM_CAP * 8
            scores = dot_t(team_rows[slot * block : slot * block + block], team_kv[slot, 0])
            scores = jnp.where(iota(scores.shape, 1) < spans[slot], scores, NEG)
            num, high, mass = softmax_part(scores, team_kv[slot, 1], scaling)
            team_num.append(num)
            team_high.append(high)
            team_mass.append(mass)
        team_num = jnp.concatenate(team_num, axis=0)
        team_high = jnp.concatenate(team_high, axis=0)
        team_mass = jnp.concatenate(team_mass, axis=0)
        eye = iota((128, 128), 0) == iota((128, 128), 1)
        high_lane = jnp.max(jnp.where(eye, team_high, NEG), axis=0, keepdims=True)
        mass_lane = jnp.sum(jnp.where(eye, team_mass, 0.0), axis=0, keepdims=True)
        coarse = team_num.astype(BF16)
        fine = (team_num - coarse.astype(F32)).astype(BF16)

        chunk = 128
        for c in range(rows // chunk):
            span_rows = pl.ds(c * chunk, chunk)
            scores = dot_t(q_all[span_rows, :], global_kv[0])
            num, high, mass = softmax_part(scores, global_kv[1], scaling)
            chosen = give[c * chunk : c * chunk + chunk]
            is_team = chosen > 0.5
            t_high = jnp.max(jnp.where(is_team, high_lane, NEG), axis=-1, keepdims=True)
            t_mass = jnp.sum(jnp.where(is_team, mass_lane, 0.0), axis=-1, keepdims=True)
            chosen = chosen.astype(BF16)
            t_num = dot(chosen, coarse) + dot(chosen, fine)
            top = jnp.maximum(high, t_high)
            g_factor = jnp.exp((high - top) * scaling)
            t_factor = jnp.exp((t_high - top) * scaling)
            mass = mass * g_factor + t_mass * t_factor
            num = (num * g_factor + t_num * t_factor) / mass
            part_out[span_rows, :] = num.astype(BF16)
            lse = jnp.where(
                iota((chunk, 128), 1) == iota((chunk, 128), 0) % 16, top * scaling + jnp.log(mass), 0.0
            )
            lse_out[pl.ds(c * chunk // 16, chunk // 16)] = jnp.sum(
                lse.reshape(chunk // 16, 16, 128), axis=1, keepdims=True
            )

        for k in range(1, chips):
            to = lax.rem(chip + k, chips)
            send(part_out.at[pl.ds(pl.multiple_of(to * 16, 16), 16)], part_in.at[own_rows], 4, peers[k - 1])
            send(lse_out.at[to], lse_in.at[chip], 5, peers[k - 1])
        keep(part_out.at[own_rows], part_in.at[own_rows], 4)
        keep(lse_out.at[chip], lse_in.at[chip], 5)
        arrived(lse_in, 5)
        lse = lse_in[...].reshape(chips, 128)
        lse = jnp.concatenate([lse, jnp.full((128 - chips, 128), NEG, F32)], axis=0).T[0:16]
        top = jnp.maximum(jnp.max(lse, axis=-1, keepdims=True), suffix_lse)
        factors = jnp.exp(lse - top)
        suffix_factor = jnp.exp(suffix_lse - top)
        total = jnp.sum(factors, axis=-1, keepdims=True) + suffix_factor
        num = suffix_num * suffix_factor
        arrived(part_in, 4)
        for j in range(chips):
            num = num + part_in[pl.ds(j * 16, 16), :].astype(F32) * factors[:, j : j + 1]
        att_own[...] = (num / total).astype(BF16)

        for peer in peers:
            send(att_own, att_all.at[own_rows], 6, peer)
        keep(att_own, att_all.at[own_rows], 6)
        local[3].wait()
        arrived(weight_hbm, 3)
        arrived(att_all, 6)
        att_f32[...] = att_all[...].astype(F32)
        att = jnp.concatenate(
            [att_f32[pl.ds(j, rows // 8, stride=8), :] for j in range(8)], axis=1
        ).astype(BF16)
        for side in range(2):
            proj_out[:, side] = dot(att, weight[side]).reshape(head_devices, rows // 8 // head_devices, 128)

        for k, d in heads:
            to = (lax.rem(h + k, head_devices), lax.rem(core + d, 2))
            send(proj_out.at[to[0], to[1]], proj_in.at[h, core], 7, head_peer(k, d))
        keep(proj_out.at[h, core], proj_in.at[h, core], 7)
        arrived(proj_in, 7)
        summed = jnp.sum(proj_in[...], axis=0)
        for side in range(2):
            for j in range(4):
                merged[pl.ds(4 * j + 2 * side, 2), :] = summed[side, 2 * j : 2 * j + 2]
        out_ref[...] = merged[...].astype(BF16)

        others = pl.ds(0, (chips - 1) * 16)
        sent(q_all.at[others], 0)
        sent(global_hbm, 1)
        sent(team_hbm, 2)
        sent(weight_hbm, 3)
        sent(part_in.at[others], 4)
        sent(lse_in.at[pl.ds(0, chips - 1)], 5)
        sent(att_all.at[others], 6)
        sent(att_f32.at[pl.ds(0, len(heads) * 8)], 7)

    return kernel, rows, chips


def shards(queries, global_kv, team_kv, suffix_kv, team_lengths, team_map, suffix_lengths, team_owner, out_weight):
    agent_devices = lax.axis_size("agents")
    head_devices = lax.axis_size("heads")
    kernel, rows, chips = make_kernel(agent_devices, head_devices)
    vmem = pl.BlockSpec(memory_space=pltpu.VMEM)
    hbm = pl.BlockSpec(memory_space=pl.ANY)
    span = global_kv.shape[1]
    out_rows = rows * 2 // 8 // head_devices
    return pl.pallas_call(
        kernel,
        out_shape=jax.ShapeDtypeStruct((out_rows, out_weight.shape[1]), BF16),
        in_specs=[vmem] * 4 + [pl.BlockSpec(memory_space=pltpu.SMEM)] + [hbm] * 4,
        out_specs=vmem,
        scratch_shapes=[
            pltpu.VMEM((16, 128), F32),
            pltpu.VMEM((16, 128), BF16),
            pltpu.VMEM((rows, 128), BF16),
            pltpu.VMEM((2, 2 * span, 128), BF16),
            pltpu.VMEM((2,) + team_kv.shape, BF16),
            pltpu.VMEM(suffix_kv.shape, BF16),
            pltpu.VMEM((2,) + out_weight.shape, BF16),
            pltpu.VMEM((rows, 128), BF16),
            pltpu.VMEM((rows, 128), BF16),
            pltpu.VMEM((chips, 1, 128), F32),
            pltpu.VMEM((chips, 1, 128), F32),
            pltpu.VMEM((16, 128), BF16),
            pltpu.VMEM((rows, 128), BF16),
            pltpu.VMEM((rows, 128), F32),
            pltpu.VMEM((head_devices, 2, 8, 128), F32),
            pltpu.VMEM((head_devices, 2, 8, 128), F32),
            pltpu.VMEM((16, 128), F32),
            pltpu.SemaphoreType.DMA((4,)),
            pltpu.SemaphoreType.DMA((8,)),
            pltpu.SemaphoreType.DMA((8,)),
        ],
        compiler_params=pltpu.CompilerParams(
            collective_id=0, has_side_effects=True, vmem_limit_bytes=48 * 1024 * 1024
        ),
        name="decode",
    )(
        queries,
        team_lengths.reshape(1, -1),
        team_map.reshape(1, -1),
        team_owner.reshape(1, -1),
        suffix_lengths,
        global_kv,
        team_kv,
        suffix_kv,
        out_weight,
    )


def solution(mesh):
    return jax.shard_map(
        shards,
        mesh=mesh,
        in_specs=(
            P("agents", "heads"),
            P(None, "agents", "heads"),
            P(None, "agents", "heads"),
            P(None, "agents", None, "heads"),
            P(),
            P(),
            P("agents"),
            P(),
            P("heads", "agents"),
        ),
        out_specs=P("heads", "agents"),
        check_vma=False,
    )
```

```python
import math

import jax
import jax.numpy as jnp
from jax import lax
from jax.experimental import pallas as pl
from jax.experimental.pallas import tpu as pltpu
from jax.sharding import PartitionSpec as P

HEAD_DIM = 128
TEAM_CAP = 8
RING = 8
NEG = -1e30
MESH = pl.DeviceIdType.MESH
F32 = jnp.float32
BF16 = jnp.bfloat16


def dot(a, b):
    return jnp.dot(a, b, preferred_element_type=F32)


def dot_t(a, b):
    return lax.dot_general(a, b, (((1,), (1,)), ((), ())), preferred_element_type=F32)


def iota(shape, dim):
    return lax.broadcasted_iota(jnp.int32, shape, dim)


def softmax_part(scores, values, scaling):
    high = jnp.max(scores, axis=-1, keepdims=True)
    weights = jnp.exp((scores - high) * scaling)
    mass = jnp.sum(weights, axis=-1, keepdims=True)
    return dot(weights.astype(BF16), values), high, mass


def make_kernel(agent_devices, head_devices):
    chips = agent_devices // 2
    rows = chips * 16

    def kernel(
        q_hbm, lengths_hbm, map_hbm, owner_hbm, suffix_len_hbm,
        global_hbm, team_hbm, suffix_hbm, weight_hbm,
        out_ref,
        q_ref, lengths_ref, map_ref, owner_ref, suffix_len_ref, q_f32, q_own, q_all, global_kv, team_kv, suffix_kv, weight,
        part_out, part_in, lse_out, lse_in, att_own, att_all, att_f32,
        proj_out, proj_in, merged,
        local_sem, send_sem, recv_sem, word,
    ):
        a = lax.axis_index("agents")
        h = lax.axis_index("heads")
        core = lax.rem(a, 2)
        chip = a // 2
        ring = RING
        lines = chips // ring
        z = lax.rem(chip, ring)
        y = chip // ring
        plane = lines * 16
        scaling = 1.0 / math.sqrt(HEAD_DIM)
        steps = [(s + 1) // 2 if s % 2 else (ring - s // 2) % ring for s in range(ring)]

        def at(dy, dz):
            return ((lax.rem(y + dy, lines) * ring + lax.rem(z + dz, ring)) * 2 + core, h)

        def head_peer(k, d):
            return (chip * 2 + lax.rem(core + d, 2), lax.rem(h + k, head_devices))

        sibling = head_peer(0, 1)
        line_peers = [at(k, 0) for k in range(1, lines)]
        ring_peers = [at(0, k) for k in range(1, ring)]
        heads = [(k, d) for k in range(head_devices) for d in range(2) if k or d]

        barrier = pltpu.get_barrier_semaphore()
        greeted = line_peers + ring_peers + [sibling]
        for peer in greeted:
            pl.semaphore_signal(barrier, inc=1, device_id=peer, device_id_type=MESH)

        @pl.when(z == 0)
        def _():
            for k in range(1, head_devices):
                pl.semaphore_signal(barrier, inc=1, device_id=head_peer(k, 0), device_id_type=MESH)

        span = global_hbm.shape[1]
        own_span = pl.ds(pl.multiple_of(core * span, span), span)
        small = [
            pltpu.make_async_copy(q_hbm, q_ref, local_sem.at[4]),
            pltpu.make_async_copy(lengths_hbm, lengths_ref, local_sem.at[5]),
            pltpu.make_async_copy(map_hbm, map_ref, local_sem.at[6]),
            pltpu.make_async_copy(owner_hbm, owner_ref, local_sem.at[7]),
            pltpu.make_async_copy(suffix_len_hbm, suffix_len_ref, local_sem.at[8]),
        ]
        local = [
            pltpu.make_async_copy(global_hbm, global_kv.at[:, own_span], local_sem.at[0]),
            pltpu.make_async_copy(team_hbm, team_kv.at[core], local_sem.at[1]),
            pltpu.make_async_copy(suffix_hbm, suffix_kv, local_sem.at[2]),
            pltpu.make_async_copy(weight_hbm, weight.at[core], local_sem.at[3]),
        ]
        for copy in small + local:
            copy.start()

        small[0].wait()
        for i in range(2):
            for j in range(8):
                q_f32[pl.ds(i * 8 + j, 1), :] = q_ref[
                    pl.ds(i, 1), pl.ds(j * HEAD_DIM, HEAD_DIM)
                ].astype(F32)
        q_own[...] = q_f32[...].astype(BF16)

        @pl.when(z == 0)
        def _():
            pl.semaphore_wait(barrier, len(greeted) + head_devices - 1)

        @pl.when(z != 0)
        def _():
            pl.semaphore_wait(barrier, len(greeted))

        own_rows = pl.ds(pl.multiple_of(chip * 16, 16), 16)
        own_line = pl.ds(pl.multiple_of(y * 16, 16), 16)

        def send(src, dst, s, peer):
            copy = pltpu.make_async_remote_copy(
                src_ref=src, dst_ref=dst, send_sem=send_sem.at[s], recv_sem=recv_sem.at[s],
                device_id=peer, device_id_type=MESH,
            )
            copy.start()

        def keep(src, dst, s):
            pltpu.make_async_copy(src, dst, recv_sem.at[s]).start()

        def arrived(ref, s):
            pltpu.make_async_copy(ref, ref, recv_sem.at[s]).wait()

        def sent(ref, s):
            pltpu.make_async_copy(ref, ref, send_sem.at[s]).wait()

        for peer in line_peers:
            send(q_own, q_all.at[own_line], 0, peer)
        keep(q_own, q_all.at[own_line], 0)
        send(global_hbm, global_kv.at[:, own_span], 1, sibling)
        send(team_hbm, team_kv.at[core], 2, sibling)
        send(weight_hbm, weight.at[core], 3, sibling)

        own_plane = q_all.at[pl.ds(0, plane)]
        arrived(own_plane, 0)
        for slot in reversed(range(1, ring)):
            there = steps.index((ring - steps[slot]) % ring)
            send(own_plane, q_all.at[pl.ds(there * plane, plane)], 8 + there // 2, at(0, steps[slot]))

        for copy in small[1:]:
            copy.wait()

        agents = map_ref.shape[1]
        team_of = map_ref[...]
        agent = iota((1, agents), 1)
        mine = lax.rem(agent // 2, 2) == core
        before = (iota((agents, agents), 0) < iota((agents, agents), 1)).astype(BF16)
        row_agent = iota((agents, rows), 1)
        slot = row_agent // plane
        step = jnp.where(slot % 2 == 1, (slot + 1) // 2, ring - slot // 2)
        row_chip = (row_agent // 16) % lines * ring + (z + step) % ring
        row_agent = row_chip * 4 + core * 2 + (row_agent // 8) % 2
        spread = (iota((agents, rows), 0) == row_agent).astype(BF16)
        owner = owner_ref[...]
        team_ids = iota(owner.shape, 1)
        picks, spans = [], []
        for slot in range(2):
            here = owner == chip * 2 + slot
            team = jnp.sum(jnp.where(here, team_ids, 0), axis=1, keepdims=True)
            spans.append(jnp.sum(jnp.where(here, lengths_ref[...], 0), axis=1, keepdims=True))
            member = jnp.logical_and(team_of == team, mine)
            members = jnp.broadcast_to(jnp.where(member, 1.0, 0.0), (8, agents)).astype(BF16)
            rank = dot(members, before)[0:1]
            code = jnp.where(member, rank, 255.0)
            picks.append(dot(jnp.broadcast_to(code, (8, agents)).astype(BF16), spread)[0:1])
        place = iota((TEAM_CAP * 8, rows), 0)
        same_head = place % 8 == iota((TEAM_CAP * 8, rows), 1) % 8
        take = jnp.concatenate(
            [
                jnp.where(
                    jnp.logical_and(code == (place // 8).astype(F32), same_head), 1.0, 0.0
                )
                for code in picks
            ],
            axis=0,
        )
        give = take.T
        take = take.astype(BF16)

        local[2].wait()
        suffix_num, suffix_lse = [], []
        for i in range(2):
            scores = dot_t(q_own[...], suffix_kv[0, i])[i * 8 : i * 8 + 8]
            seen = iota(scores.shape, 1) < suffix_len_ref[i]
            high = jnp.max(jnp.where(seen, scores, NEG), axis=-1, keepdims=True)
            weights = jnp.where(seen, jnp.exp((jnp.minimum(scores, high) - high) * scaling), 0.0)
            mass = jnp.sum(weights, axis=-1, keepdims=True)
            weights = jnp.concatenate([weights, weights], axis=0).astype(BF16)
            num = dot(weights, suffix_kv[1, i])[0:8]
            suffix_num.append(num / mass)
            suffix_lse.append(high * scaling + jnp.log(mass))
        suffix_num = jnp.concatenate(suffix_num, axis=0)
        suffix_lse = jnp.concatenate(suffix_lse, axis=0)

        chunk = 2 * plane
        chunks = rows // chunk
        local[0].wait()
        arrived(global_hbm, 1)
        prompt = []
        for c in range(chunks):
            first = c * chunk + (plane if c == 0 else 0)
            arrived(q_all.at[pl.ds(first, (c + 1) * chunk - first)], 8 + c)
            scores = dot_t(q_all[pl.ds(c * chunk, chunk), :], global_kv[0])
            prompt.append(softmax_part(scores, global_kv[1], scaling))

        local[1].wait()
        arrived(team_hbm, 2)
        team_rows = dot(take, q_all[...]).astype(BF16)
        team_num, team_high, team_mass = [], [], []
        for slot in range(2):
            block = TEAM_CAP * 8
            scores = dot_t(team_rows[slot * block : slot * block + block], team_kv[slot, 0])
            scores = jnp.where(iota(scores.shape, 1) < spans[slot], scores, NEG)
            num, high, mass = softmax_part(scores, team_kv[slot, 1], scaling)
            team_num.append(num)
            team_high.append(high)
            team_mass.append(mass)
        team_num = jnp.concatenate(team_num, axis=0)
        team_high = jnp.concatenate(team_high, axis=0)
        team_mass = jnp.concatenate(team_mass, axis=0)
        eye = iota((128, 128), 0) == iota((128, 128), 1)
        high_lane = jnp.max(jnp.where(eye, team_high, NEG), axis=0, keepdims=True)
        mass_lane = jnp.sum(jnp.where(eye, team_mass, 0.0), axis=0, keepdims=True)
        coarse = team_num.astype(BF16)
        fine = (team_num - coarse.astype(F32)).astype(BF16)

        for c in range(chunks):
            span_rows = pl.ds(c * chunk, chunk)
            num, high, mass = prompt[c]
            chosen = give[c * chunk : c * chunk + chunk]
            is_team = chosen > 0.5
            t_high = jnp.max(jnp.where(is_team, high_lane, NEG), axis=-1, keepdims=True)
            t_mass = jnp.sum(jnp.where(is_team, mass_lane, 0.0), axis=-1, keepdims=True)
            chosen = chosen.astype(BF16)
            t_num = dot(chosen, coarse) + dot(chosen, fine)
            top = jnp.maximum(high, t_high)
            g_factor = jnp.exp((high - top) * scaling)
            t_factor = jnp.exp((t_high - top) * scaling)
            mass = mass * g_factor + t_mass * t_factor
            num = (num * g_factor + t_num * t_factor) / mass
            part_out[span_rows, :] = num.astype(BF16)
            lse = jnp.where(
                iota((chunk, 128), 1) == iota((chunk, 128), 0) % 16, top * scaling + jnp.log(mass), 0.0
            )
            lse_out[pl.ds(c * chunk // 16, chunk // 16)] = jnp.sum(
                lse.reshape(chunk // 16, 16, 128), axis=1, keepdims=True
            )

        for slot in reversed(range(ring)):
            for k in reversed(range(lines)):
                if slot or k:
                    block = slot * lines + lax.rem(y + k, lines)
                    peer = at(k, steps[slot])
                    send(part_out.at[pl.ds(pl.multiple_of(block * 16, 16), 16)], part_in.at[own_rows], 4, peer)
                    send(lse_out.at[block], lse_in.at[chip], 5, peer)
        keep(part_out.at[own_line], part_in.at[own_rows], 4)
        keep(lse_out.at[y], lse_in.at[chip], 5)

        arrived(lse_in, 5)
        lse = lse_in[...].reshape(chips, 128)
        lse = jnp.concatenate([lse, jnp.full((128 - chips, 128), NEG, F32)], axis=0).T[0:16]
        top = jnp.maximum(jnp.max(lse, axis=-1, keepdims=True), suffix_lse)
        factors = jnp.exp(lse - top)
        suffix_factor = jnp.exp(suffix_lse - top)
        total = jnp.sum(factors, axis=-1, keepdims=True) + suffix_factor
        num = suffix_num * suffix_factor
        arrived(part_in, 4)
        for j in range(chips):
            num = num + part_in[pl.ds(j * 16, 16), :].astype(F32) * factors[:, j : j + 1]
        att_own[...] = (num / total).astype(BF16)

        for slot in reversed(range(ring)):
            for k in reversed(range(lines)):
                if slot or k:
                    send(att_own, att_all.at[own_rows], 6, at(k, steps[slot]))
        keep(att_own, att_all.at[own_rows], 6)

        @pl.when(z == 0)
        def _():
            for k in range(1, head_devices):
                pl.semaphore_signal(word.at[0], inc=1, device_id=head_peer(k, 0), device_id_type=MESH)
            pl.semaphore_wait(word.at[0], head_devices - 1)
            for peer in ring_peers:
                pl.semaphore_signal(word.at[1], inc=1, device_id=peer, device_id_type=MESH)

        local[3].wait()
        arrived(weight_hbm, 3)
        arrived(att_all, 6)
        att_f32[...] = att_all[...].astype(F32)
        att = jnp.concatenate(
            [att_f32[pl.ds(j, rows // 8, stride=8), :] for j in range(8)], axis=1
        ).astype(BF16)
        for side in range(2):
            proj_out[pl.ds(side * head_devices, head_devices)] = (
                dot(att, weight[side]).astype(BF16).reshape(head_devices, 8, 128)
            )

        @pl.when(z != 0)
        def _():
            pl.semaphore_wait(word.at[1], 1)

        for k, d in heads:
            to = (lax.rem(h + k, head_devices), lax.rem(core + d, 2))
            send(proj_out.at[to[1] * head_devices + to[0]], proj_in.at[core * head_devices + h], 7, head_peer(k, d))
        keep(proj_out.at[core * head_devices + h], proj_in.at[core * head_devices + h], 7)
        arrived(proj_in, 7)
        for side in range(2):
            summed = jnp.sum(proj_in[pl.ds(side * head_devices, head_devices)].astype(F32), axis=0)
            for j in range(4):
                merged[pl.ds(4 * j + 2 * side, 2), :] = summed[2 * j : 2 * j + 2]
        out_ref[...] = merged[...].astype(BF16)

        others = pl.ds(0, (chips - 1) * 16)
        sent(q_all.at[pl.ds(0, plane - 16)], 0)
        for c in range(chunks):
            first = c * chunk + (plane if c == 0 else 0)
            sent(q_all.at[pl.ds(first, (c + 1) * chunk - first)], 8 + c)
        sent(global_hbm, 1)
        sent(team_hbm, 2)
        sent(weight_hbm, 3)
        sent(part_in.at[others], 4)
        sent(lse_in.at[pl.ds(0, chips - 1)], 5)
        sent(att_all.at[others], 6)
        sent(proj_in.at[pl.ds(0, len(heads))], 7)

    return kernel, rows, chips


def shards(queries, global_kv, team_kv, suffix_kv, team_lengths, team_map, suffix_lengths, team_owner, out_weight):
    agent_devices = lax.axis_size("agents")
    head_devices = lax.axis_size("heads")
    kernel, rows, chips = make_kernel(agent_devices, head_devices)
    vmem = pl.BlockSpec(memory_space=pltpu.VMEM)
    hbm = pl.BlockSpec(memory_space=pltpu.HBM)
    span = global_kv.shape[1]
    out_rows = rows * 2 // 8 // head_devices
    return pl.pallas_call(
        kernel,
        out_shape=pltpu.VMEM((out_rows, out_weight.shape[1]), BF16),
        in_specs=[hbm] * 9,
        out_specs=vmem,
        scratch_shapes=[
            pltpu.VMEM(queries.shape, BF16),
            pltpu.VMEM((1,) + team_lengths.shape, jnp.int32),
            pltpu.VMEM((1,) + team_map.shape, jnp.int32),
            pltpu.VMEM((1,) + team_owner.shape, jnp.int32),
            pltpu.SMEM(suffix_lengths.shape, jnp.int32),
            pltpu.VMEM((16, 128), F32),
            pltpu.VMEM((16, 128), BF16),
            pltpu.VMEM((rows, 128), BF16),
            pltpu.VMEM((2, 2 * span, 128), BF16),
            pltpu.VMEM((2,) + team_kv.shape, BF16),
            pltpu.VMEM(suffix_kv.shape, BF16),
            pltpu.VMEM((2,) + out_weight.shape, BF16),
            pltpu.VMEM((rows, 128), BF16),
            pltpu.VMEM((rows, 128), BF16),
            pltpu.VMEM((chips, 1, 128), F32),
            pltpu.VMEM((chips, 1, 128), F32),
            pltpu.VMEM((16, 128), BF16),
            pltpu.VMEM((rows, 128), BF16),
            pltpu.VMEM((rows, 128), F32),
            pltpu.VMEM((2 * head_devices, 8, 128), BF16),
            pltpu.VMEM((2 * head_devices, 8, 128), BF16),
            pltpu.VMEM((16, 128), F32),
            pltpu.SemaphoreType.DMA((9,)),
            pltpu.SemaphoreType.DMA((12,)),
            pltpu.SemaphoreType.DMA((12,)),
            pltpu.SemaphoreType.REGULAR((2,)),
        ],
        compiler_params=pltpu.CompilerParams(
            collective_id=0, has_side_effects=True, vmem_limit_bytes=62 * 1024 * 1024
        ),
        name="decode",
    )(
        queries,
        team_lengths.reshape(1, -1),
        team_map.reshape(1, -1),
        team_owner.reshape(1, -1),
        suffix_lengths,
        global_kv,
        team_kv,
        suffix_kv,
        out_weight,
    )


def solution(mesh):
    return jax.shard_map(
        shards,
        mesh=mesh,
        in_specs=(
            P("agents", "heads"),
            P(None, "agents", "heads"),
            P(None, "agents", "heads"),
            P(None, "agents", None, "heads"),
            P(),
            P(),
            P("agents"),
            P(),
            P("heads", "agents"),
        ),
        out_specs=P("heads", "agents"),
        check_vma=False,
    )
```

```python
import math

import jax
import jax.numpy as jnp
from jax import lax
from jax.experimental import pallas as pl
from jax.experimental.pallas import tpu as pltpu
from jax.sharding import PartitionSpec as P

HEAD_DIM = 128
TEAM_CAP = 8
RING = 8
NEG = -1e30
MESH = pl.DeviceIdType.MESH
F32 = jnp.float32
BF16 = jnp.bfloat16


def dot(a, b):
    return jnp.dot(a, b, preferred_element_type=F32)


def dot_t(a, b):
    return lax.dot_general(a, b, (((1,), (1,)), ((), ())), preferred_element_type=F32)


def iota(shape, dim):
    return lax.broadcasted_iota(jnp.int32, shape, dim)


def softmax_part(scores, values, scaling):
    high = jnp.max(scores, axis=-1, keepdims=True)
    weights = jnp.exp((scores - high) * scaling)
    mass = jnp.sum(weights, axis=-1, keepdims=True)
    return dot(weights.astype(BF16), values), high, mass


def fold(first, second):
    top = jnp.maximum(first[1], second[1])
    one, two = jnp.exp(first[1] - top), jnp.exp(second[1] - top)
    total = one + two
    return first[0] * (one / total) + second[0] * (two / total), top + jnp.log(total)


def make_kernel(agent_devices, head_devices):
    chips = agent_devices // 2
    rows = chips * 16

    def kernel(
        q_hbm, lengths_hbm, map_hbm, owner_hbm, suffix_len_hbm,
        global_hbm, team_hbm, suffix_hbm, weight_hbm,
        out_ref,
        q_ref, lengths_ref, map_ref, owner_ref, suffix_len_ref, q_f32, q_own, q_all, global_kv, team_kv, suffix_kv, weight,
        part_out, part_in, lse_out, lse_in, att_own, att_all, att_f32,
        proj_out, proj_in, merged,
        local_sem, send_sem, recv_sem, word, above,
    ):
        a = lax.axis_index("agents")
        h = lax.axis_index("heads")
        core = lax.rem(a, 2)
        chip = a // 2
        ring = RING
        lines = chips // ring
        z = lax.rem(chip, ring)
        y = chip // ring
        plane = lines * 16
        scaling = 1.0 / math.sqrt(HEAD_DIM)
        steps = [(s + 1) // 2 if s % 2 else (ring - s // 2) % ring for s in range(ring)]

        def at(dy, dz):
            return ((lax.rem(y + dy, lines) * ring + lax.rem(z + dz, ring)) * 2 + core, h)

        def head_peer(k, d):
            return (chip * 2 + lax.rem(core + d, 2), lax.rem(h + k, head_devices))

        sibling = head_peer(0, 1)
        line_peers = [at(k, 0) for k in range(1, lines)]
        ring_peers = [at(0, k) for k in range(1, ring)]
        heads = [(k, d) for k in range(head_devices) for d in range(2) if k or d]

        barrier = pltpu.get_barrier_semaphore()

        def hello(peer):
            pl.semaphore_signal(barrier, inc=1, device_id=peer, device_id_type=MESH)

        for peer in line_peers + [sibling]:
            hello(peer)

        @pl.when(z > 0)
        def _():
            hello(at(0, ring - 1))

        for off in range(1, ring):
            @pl.when(z + off < ring)
            def _(off=off):
                for k in range(lines):
                    hello(at(k, off))

        @pl.when(z == 0)
        def _():
            for k in range(1, head_devices):
                hello(head_peer(k, 0))

        span = global_hbm.shape[1]
        own_span = pl.ds(pl.multiple_of(core * span, span), span)
        small = [
            pltpu.make_async_copy(q_hbm, q_ref, local_sem.at[4]),
            pltpu.make_async_copy(lengths_hbm, lengths_ref, local_sem.at[5]),
            pltpu.make_async_copy(map_hbm, map_ref, local_sem.at[6]),
            pltpu.make_async_copy(owner_hbm, owner_ref, local_sem.at[7]),
            pltpu.make_async_copy(suffix_len_hbm, suffix_len_ref, local_sem.at[8]),
        ]
        local = [
            pltpu.make_async_copy(global_hbm, global_kv.at[:, own_span], local_sem.at[0]),
            pltpu.make_async_copy(team_hbm, team_kv.at[core], local_sem.at[1]),
            pltpu.make_async_copy(suffix_hbm, suffix_kv, local_sem.at[2]),
            pltpu.make_async_copy(weight_hbm, weight.at[core], local_sem.at[3]),
        ]
        for copy in small + local:
            copy.start()

        small[0].wait()
        for i in range(2):
            for j in range(8):
                q_f32[pl.ds(i * 8 + j, 1), :] = q_ref[
                    pl.ds(i, 1), pl.ds(j * HEAD_DIM, HEAD_DIM)
                ].astype(F32)
        q_own[...] = q_f32[...].astype(BF16)

        top_plane = (z + 1) // ring
        bottom_plane = 1 - (z + ring - 1) // ring
        pl.semaphore_wait(
            barrier, lines * (z + 1) + 1 - top_plane + (head_devices - 1) * bottom_plane
        )

        own_rows = pl.ds(pl.multiple_of(chip * 16, 16), 16)
        own_line = pl.ds(pl.multiple_of(y * 16, 16), 16)

        def send(src, dst, s, peer):
            copy = pltpu.make_async_remote_copy(
                src_ref=src, dst_ref=dst, send_sem=send_sem.at[s], recv_sem=recv_sem.at[s],
                device_id=peer, device_id_type=MESH,
            )
            copy.start()

        def keep(src, dst, s):
            pltpu.make_async_copy(src, dst, recv_sem.at[s]).start()

        def arrived(ref, s):
            pltpu.make_async_copy(ref, ref, recv_sem.at[s]).wait()

        def sent(ref, s):
            pltpu.make_async_copy(ref, ref, send_sem.at[s]).wait()

        for peer in line_peers:
            send(q_own, q_all.at[own_line], 0, peer)
        keep(q_own, q_all.at[own_line], 0)

        def landing_slot(slot):
            return steps.index((ring - steps[slot]) % ring)

        for slot in reversed(range(1, ring)):
            off, there = steps[slot], landing_slot(slot)

            @pl.when(z + off >= ring)
            def _(off=off, there=there):
                rows_there = pl.ds(pl.multiple_of(there * plane + y * 16, 16), 16)
                for k in reversed(range(lines)):
                    send(q_own, q_all.at[rows_there], 8 + there // 2, at(k, off))

        @pl.when(z < ring - 1)
        def _():
            for off in range(1, ring):
                @pl.when(z >= off)
                def _(off=off):
                    pl.semaphore_signal(
                        above.at[z + 1], inc=1, device_id=at(0, ring - off), device_id_type=MESH
                    )

        send(global_hbm, global_kv.at[:, own_span], 1, sibling)
        send(team_hbm, team_kv.at[core], 2, sibling)
        send(weight_hbm, weight.at[core], 3, sibling)

        for copy in small[1:]:
            copy.wait()

        agents = map_ref.shape[1]
        team_of = map_ref[...]
        agent = iota((1, agents), 1)
        mine = lax.rem(agent // 2, 2) == core
        before = (iota((agents, agents), 0) < iota((agents, agents), 1)).astype(BF16)
        row_agent = iota((agents, rows), 1)
        slot = row_agent // plane
        step = jnp.where(slot % 2 == 1, (slot + 1) // 2, ring - slot // 2)
        row_chip = (row_agent // 16) % lines * ring + (z + step) % ring
        row_agent = row_chip * 4 + core * 2 + (row_agent // 8) % 2
        spread = (iota((agents, rows), 0) == row_agent).astype(BF16)
        owner = owner_ref[...]
        team_ids = iota(owner.shape, 1)
        picks, spans = [], []
        for slot in range(2):
            here = owner == chip * 2 + slot
            team = jnp.sum(jnp.where(here, team_ids, 0), axis=1, keepdims=True)
            spans.append(jnp.sum(jnp.where(here, lengths_ref[...], 0), axis=1, keepdims=True))
            member = jnp.logical_and(team_of == team, mine)
            members = jnp.broadcast_to(jnp.where(member, 1.0, 0.0), (8, agents)).astype(BF16)
            rank = dot(members, before)[0:1]
            code = jnp.where(member, rank, 255.0)
            picks.append(dot(jnp.broadcast_to(code, (8, agents)).astype(BF16), spread)[0:1])
        place = iota((TEAM_CAP * 8, rows), 0)
        same_head = place % 8 == iota((TEAM_CAP * 8, rows), 1) % 8
        take = jnp.concatenate(
            [
                jnp.where(
                    jnp.logical_and(code == (place // 8).astype(F32), same_head), 1.0, 0.0
                )
                for code in picks
            ],
            axis=0,
        )
        give = take.T
        is_team = give > 0.5
        give = give.astype(BF16)
        take = take.astype(BF16)

        local[2].wait()
        suffix_num, suffix_lse = [], []
        for i in range(2):
            scores = dot_t(q_own[...], suffix_kv[0, i])[i * 8 : i * 8 + 8]
            seen = iota(scores.shape, 1) < suffix_len_ref[i]
            high = jnp.max(jnp.where(seen, scores, NEG), axis=-1, keepdims=True)
            weights = jnp.where(seen, jnp.exp((jnp.minimum(scores, high) - high) * scaling), 0.0)
            mass = jnp.sum(weights, axis=-1, keepdims=True)
            weights = jnp.concatenate([weights, weights], axis=0).astype(BF16)
            num = dot(weights, suffix_kv[1, i])[0:8]
            suffix_num.append(num / mass)
            suffix_lse.append(high * scaling + jnp.log(mass))
        suffix_num = jnp.concatenate(suffix_num, axis=0)
        suffix_lse = jnp.concatenate(suffix_lse, axis=0)
        others = rows // RING * 2 - plane
        suffix_num = jnp.concatenate([suffix_num] * lines + [jnp.zeros((others, 128), F32)], axis=0)
        suffix_lse = jnp.concatenate(
            [jnp.where(y == j, suffix_lse, NEG) for j in range(lines)]
            + [jnp.full((others, 1), NEG, F32)],
            axis=0,
        )

        own_plane = q_all.at[pl.ds(0, plane)]
        arrived(own_plane, 0)
        for off in range(1, ring):
            there = landing_slot(steps.index(off))

            @pl.when(z + off < ring)
            def _(off=off, there=there):
                if off > 1:
                    pl.semaphore_wait(above.at[z + off], 1)
                send(own_plane, q_all.at[pl.ds(there * plane, plane)], 8 + there // 2, at(0, off))

        chunk = 2 * plane
        chunks = rows // chunk
        local[0].wait()
        arrived(global_hbm, 1)
        prompt = []
        for c in range(chunks):
            first = c * chunk + (plane if c == 0 else 0)
            arrived(q_all.at[pl.ds(first, (c + 1) * chunk - first)], 8 + c)
            scores = dot_t(q_all[pl.ds(c * chunk, chunk), :], global_kv[0])
            num, high, mass = softmax_part(scores, global_kv[1], scaling)
            part = num / mass, high * scaling + jnp.log(mass)
            if c == 0:
                part = fold(part, (suffix_num, suffix_lse))
            prompt.append(part)

        @pl.when(z == 0)
        def _():
            for k in range(1, head_devices):
                pl.semaphore_signal(word.at[0], inc=1, device_id=head_peer(k, 0), device_id_type=MESH)

        local[1].wait()
        arrived(team_hbm, 2)
        team_rows = dot(take, q_all[...]).astype(BF16)
        team_num, team_lse = [], []
        for slot in range(2):
            block = TEAM_CAP * 8
            scores = dot_t(team_rows[slot * block : slot * block + block], team_kv[slot, 0])
            scores = jnp.where(iota(scores.shape, 1) < spans[slot], scores, NEG)
            num, high, mass = softmax_part(scores, team_kv[slot, 1], scaling)
            team_num.append(num / mass)
            team_lse.append(high * scaling + jnp.log(mass))
        team_num = jnp.concatenate(team_num, axis=0)
        team_lse = jnp.concatenate(team_lse, axis=0)
        eye = iota((128, 128), 0) == iota((128, 128), 1)
        lse_lane = jnp.max(jnp.where(eye, team_lse, NEG), axis=0, keepdims=True)
        coarse = team_num.astype(BF16)
        team_num = jnp.concatenate([coarse, (team_num - coarse.astype(F32)).astype(BF16)], axis=1)

        for c in range(chunks):
            span_rows = pl.ds(c * chunk, chunk)
            num = dot(give[c * chunk : c * chunk + chunk], team_num)
            lse = jnp.where(is_team[c * chunk : c * chunk + chunk], lse_lane, NEG)
            lse = jnp.max(lse, axis=-1, keepdims=True)
            num, lse = fold(prompt[c], (num[:, :128] + num[:, 128:], lse))
            part_out[span_rows, :] = num.astype(BF16)
            lse = jnp.where(
                iota((chunk, 128), 1) == iota((chunk, 128), 0) % 16, lse, 0.0
            )
            lse_out[pl.ds(c * chunk // 16, chunk // 16)] = jnp.sum(
                lse.reshape(chunk // 16, 16, 128), axis=1, keepdims=True
            )

        far_side = lax.rem(h, 2)

        def block_of(line, at_ring):
            middle = (line + 1) // 2 % 2
            row_line = line // 2 * 2 + at_ring // 4
            off = (at_ring % 4 + 4 * ((far_side + middle) % 2) - z + ring) % ring
            some, back = (off + ring - 1) // ring, (off + ring // 2 - 1) // ring
            slot = (1 - back) * (2 * off - some) + back * 2 * (ring - off)
            return slot * lines + row_line

        for slot in reversed(range(ring)):
            for k in reversed(range(lines)):
                if slot or k:
                    block = block_of(lax.rem(y + k, lines), lax.rem(z + steps[slot], ring))
                    peer = at(k, steps[slot])
                    send(part_out.at[pl.ds(pl.multiple_of(block * 16, 16), 16)], part_in.at[own_rows], 4, peer)
                    send(lse_out.at[block], lse_in.at[chip], 5, peer)
        block = block_of(y, z)
        keep(part_out.at[pl.ds(pl.multiple_of(block * 16, 16), 16)], part_in.at[own_rows], 4)
        keep(lse_out.at[block], lse_in.at[chip], 5)
        arrived(lse_in, 5)
        lse = lse_in[...].reshape(chips, 128)
        lse = jnp.concatenate([lse, jnp.full((128 - chips, 128), NEG, F32)], axis=0).T[0:16]
        factors = jnp.exp(lse - jnp.max(lse, axis=-1, keepdims=True))
        factors = factors / jnp.sum(factors, axis=-1, keepdims=True)
        arrived(part_in, 4)
        num = part_in[pl.ds(0, 16), :].astype(F32) * factors[:, 0:1]
        for j in range(1, chips):
            num = num + part_in[pl.ds(j * 16, 16), :].astype(F32) * factors[:, j : j + 1]
        att_own[...] = num.astype(BF16)

        kind = 12 + (y + 1) // 2 % 2
        for slot in reversed(range(ring)):
            for k in reversed(range(lines)):
                if slot or k:
                    send(att_own, att_all.at[own_rows], kind, at(k, steps[slot]))
        keep(att_own, att_all.at[own_rows], kind)

        @pl.when(z == 0)
        def _():
            pl.semaphore_wait(word.at[0], head_devices - 1)
            for peer in ring_peers:
                pl.semaphore_signal(word.at[1], inc=1, device_id=peer, device_id_type=MESH)

        local[3].wait()
        arrived(weight_hbm, 3)

        def project(spans, units):
            parts = []
            for start, size in spans:
                att_f32[pl.ds(start, size), :] = att_all[pl.ds(start, size), :].astype(F32)
            for j in range(8):
                parts.append(
                    jnp.concatenate(
                        [att_f32[pl.ds(start + j, size // 8, stride=8), :] for start, size in spans], axis=0
                    )
                )
            att = jnp.concatenate(parts, axis=1).astype(BF16)
            for side in range(2):
                sums = dot(att, weight[side]).astype(BF16).reshape(len(units), 8, 128)
                for n, unit in enumerate(units):
                    proj_out[side * head_devices + unit] = sums[n]

        def to_heads(side_of, unit_of):
            for k in range(head_devices // 2):
                line = lax.rem(h // 2 + k, head_devices // 2)
                there = line * 2 + side_of
                for d in range(2):
                    to_core = lax.rem(core + d, 2)
                    src = proj_out.at[to_core * head_devices + unit_of(line)]
                    yield k, d, src, (chip * 2 + to_core, there)

        arrived(att_all.at[pl.ds(0, rows // 2)], 13)
        project([(rows // 4, rows // 2)], [2, 3, 4, 5])

        @pl.when(z != 0)
        def _():
            pl.semaphore_wait(word.at[1], 1)

        landing = proj_in.at[core * head_devices + h]
        for k, d, src, peer in to_heads(1 - far_side, lambda line: 2 + line):
            send(src, landing, 7, peer)
        arrived(att_all.at[pl.ds(0, rows // 2)], 12)
        project([(0, rows // 4), (3 * rows // 4, rows // 4)], [0, 1, 6, 7])
        for k, d, src, peer in to_heads(far_side, lambda line: line // 2 * 6 + line % 2):
            if k or d:
                send(src, landing, 7, peer)
            else:
                keep(src, landing, 7)
        arrived(proj_in, 7)
        for side in range(2):
            summed = jnp.sum(proj_in[pl.ds(side * head_devices, head_devices)].astype(F32), axis=0)
            for j in range(4):
                merged[pl.ds(4 * j + 2 * side, 2), :] = summed[2 * j : 2 * j + 2]
        out_ref[...] = merged[...].astype(BF16)

        others = pl.ds(0, (chips - 1) * 16)
        sent(q_all.at[pl.ds(0, plane - 16)], 0)
        for c in range(chunks):
            first = c * chunk + (plane if c == 0 else 0)
            sent(q_all.at[pl.ds(first, (c + 1) * chunk - first)], 8 + c)
        sent(global_hbm, 1)
        sent(team_hbm, 2)
        sent(weight_hbm, 3)
        sent(part_in.at[others], 4)
        sent(lse_in.at[pl.ds(0, chips - 1)], 5)
        sent(att_all.at[others], kind)
        sent(proj_in.at[pl.ds(0, len(heads))], 7)

    return kernel, rows, chips


def shards(queries, global_kv, team_kv, suffix_kv, team_lengths, team_map, suffix_lengths, team_owner, out_weight):
    agent_devices = lax.axis_size("agents")
    head_devices = lax.axis_size("heads")
    kernel, rows, chips = make_kernel(agent_devices, head_devices)
    vmem = pl.BlockSpec(memory_space=pltpu.VMEM)
    hbm = pl.BlockSpec(memory_space=pltpu.HBM)
    span = global_kv.shape[1]
    out_rows = rows * 2 // 8 // head_devices
    return pl.pallas_call(
        kernel,
        out_shape=pltpu.VMEM((out_rows, out_weight.shape[1]), BF16),
        in_specs=[hbm] * 9,
        out_specs=vmem,
        scratch_shapes=[
            pltpu.VMEM(queries.shape, BF16),
            pltpu.VMEM((1,) + team_lengths.shape, jnp.int32),
            pltpu.VMEM((1,) + team_map.shape, jnp.int32),
            pltpu.VMEM((1,) + team_owner.shape, jnp.int32),
            pltpu.SMEM(suffix_lengths.shape, jnp.int32),
            pltpu.VMEM((16, 128), F32),
            pltpu.VMEM((16, 128), BF16),
            pltpu.VMEM((rows, 128), BF16),
            pltpu.VMEM((2, 2 * span, 128), BF16),
            pltpu.VMEM((2,) + team_kv.shape, BF16),
            pltpu.VMEM(suffix_kv.shape, BF16),
            pltpu.VMEM((2,) + out_weight.shape, BF16),
            pltpu.VMEM((rows, 128), BF16),
            pltpu.VMEM((rows, 128), BF16),
            pltpu.VMEM((chips, 1, 128), F32),
            pltpu.VMEM((chips, 1, 128), F32),
            pltpu.VMEM((16, 128), BF16),
            pltpu.VMEM((rows, 128), BF16),
            pltpu.VMEM((rows, 128), F32),
            pltpu.VMEM((2 * head_devices, 8, 128), BF16),
            pltpu.VMEM((2 * head_devices, 8, 128), BF16),
            pltpu.VMEM((16, 128), F32),
            pltpu.SemaphoreType.DMA((9,)),
            pltpu.SemaphoreType.DMA((14,)),
            pltpu.SemaphoreType.DMA((14,)),
            pltpu.SemaphoreType.REGULAR((2,)),
            pltpu.SemaphoreType.REGULAR((RING,)),
        ],
        compiler_params=pltpu.CompilerParams(
            collective_id=0, has_side_effects=True, vmem_limit_bytes=62 * 1024 * 1024
        ),
        name="decode",
    )(
        queries,
        team_lengths.reshape(1, -1),
        team_map.reshape(1, -1),
        team_owner.reshape(1, -1),
        suffix_lengths,
        global_kv,
        team_kv,
        suffix_kv,
        out_weight,
    )


def solution(mesh):
    return jax.shard_map(
        shards,
        mesh=mesh,
        in_specs=(
            P("agents", "heads"),
            P(None, "agents", "heads"),
            P(None, "agents", "heads"),
            P(None, "agents", None, "heads"),
            P(),
            P(),
            P("agents"),
            P(),
            P("heads", "agents"),
        ),
        out_specs=P("heads", "agents"),
        check_vma=False,
    )
```

```python
import math

import jax
import jax.numpy as jnp
from jax import lax
from jax.experimental import pallas as pl
from jax.experimental.pallas import tpu as pltpu
from jax.sharding import PartitionSpec as P

HEAD_DIM = 128
TEAM_CAP = 8
RING = 8
NEG = -1e30
LOG2E = math.log2(math.e)
MESH = pl.DeviceIdType.MESH
F32 = jnp.float32
BF16 = jnp.bfloat16


def dot(a, b):
    return jnp.dot(a, b, preferred_element_type=F32)


def dot_t(a, b):
    return lax.dot_general(a, b, (((1,), (1,)), ((), ())), preferred_element_type=F32)


def iota(shape, dim):
    return lax.broadcasted_iota(jnp.int32, shape, dim)


def softmax_part(scores, values, scaling):
    high = jnp.max(scores, axis=-1, keepdims=True)
    weights = jnp.exp2((scores - high) * (scaling * LOG2E))
    mass = jnp.sum(weights, axis=-1, keepdims=True)
    return dot(weights.astype(BF16), values), high, mass


def fold(first, second):
    top = jnp.maximum(first[1], second[1])
    one, two = jnp.exp(first[1] - top), jnp.exp(second[1] - top)
    total = one + two
    return first[0] * (one / total) + second[0] * (two / total), top + jnp.log(total)


def make_kernel(agent_devices, head_devices):
    chips = agent_devices // 2
    rows = chips * 16

    def kernel(
        q_hbm, lengths_hbm, map_hbm, owner_hbm, suffix_len_hbm,
        global_hbm, team_hbm, suffix_hbm, weight_hbm,
        out_ref,
        q_ref, lengths_ref, map_ref, owner_ref, suffix_len_ref, q_f32, q_own, q_all, global_kv, team_kv, suffix_kv, weight,
        part_out, part_in, lse_out, lse_in, att_own, att_all, att_f32,
        proj_out, proj_in, merged,
        local_sem, send_sem, recv_sem, word, above,
    ):
        a = lax.axis_index("agents")
        h = lax.axis_index("heads")
        core = lax.rem(a, 2)
        chip = a // 2
        ring = RING
        lines = chips // ring
        z = lax.rem(chip, ring)
        y = chip // ring
        plane = lines * 16
        scaling = 1.0 / math.sqrt(HEAD_DIM)
        steps = [(s + 1) // 2 if s % 2 else (ring - s // 2) % ring for s in range(ring)]

        def at(dy, dz):
            return ((lax.rem(y + dy, lines) * ring + lax.rem(z + dz, ring)) * 2 + core, h)

        def head_peer(k, d):
            return (chip * 2 + lax.rem(core + d, 2), lax.rem(h + k, head_devices))

        sibling = head_peer(0, 1)
        line_peers = [at(k, 0) for k in range(1, lines)]
        ring_peers = [at(0, k) for k in range(1, ring)]
        heads = [(k, d) for k in range(head_devices) for d in range(2) if k or d]

        barrier = pltpu.get_barrier_semaphore()

        def hello(peer):
            pl.semaphore_signal(barrier, inc=1, device_id=peer, device_id_type=MESH)

        for peer in line_peers + [sibling]:
            hello(peer)

        @pl.when(z > 0)
        def _():
            hello(at(0, ring - 1))

        for off in range(1, ring):
            @pl.when(z + off < ring)
            def _(off=off):
                for k in range(lines):
                    hello(at(k, off))

        @pl.when(z == 0)
        def _():
            for k in range(1, head_devices):
                hello(head_peer(k, 0))

        span = global_hbm.shape[1]
        own_span = pl.ds(pl.multiple_of(core * span, span), span)
        small = [
            pltpu.make_async_copy(q_hbm, q_ref, local_sem.at[4]),
            pltpu.make_async_copy(lengths_hbm, lengths_ref, local_sem.at[5]),
            pltpu.make_async_copy(map_hbm, map_ref, local_sem.at[6]),
            pltpu.make_async_copy(owner_hbm, owner_ref, local_sem.at[7]),
            pltpu.make_async_copy(suffix_len_hbm, suffix_len_ref, local_sem.at[8]),
        ]
        local = [
            pltpu.make_async_copy(global_hbm, global_kv.at[:, own_span], local_sem.at[0]),
            pltpu.make_async_copy(team_hbm, team_kv.at[core], local_sem.at[1]),
            pltpu.make_async_copy(suffix_hbm, suffix_kv, local_sem.at[2]),
            pltpu.make_async_copy(weight_hbm, weight.at[core], local_sem.at[3]),
        ]
        for copy in small + local:
            copy.start()

        small[0].wait()
        for i in range(2):
            for j in range(8):
                q_f32[pl.ds(i * 8 + j, 1), :] = q_ref[
                    pl.ds(i, 1), pl.ds(j * HEAD_DIM, HEAD_DIM)
                ].astype(F32)
        q_own[...] = q_f32[...].astype(BF16)

        top_plane = (z + 1) // ring
        bottom_plane = 1 - (z + ring - 1) // ring
        pl.semaphore_wait(
            barrier, lines * (z + 1) + 1 - top_plane + (head_devices - 1) * bottom_plane
        )

        own_rows = pl.ds(pl.multiple_of(chip * 16, 16), 16)
        own_line = pl.ds(pl.multiple_of(y * 16, 16), 16)

        def send(src, dst, s, peer):
            copy = pltpu.make_async_remote_copy(
                src_ref=src, dst_ref=dst, send_sem=send_sem.at[s], recv_sem=recv_sem.at[s],
                device_id=peer, device_id_type=MESH,
            )
            copy.start()

        def keep(src, dst, s):
            pltpu.make_async_copy(src, dst, recv_sem.at[s]).start()

        def arrived(ref, s):
            pltpu.make_async_copy(ref, ref, recv_sem.at[s]).wait()

        def sent(ref, s):
            pltpu.make_async_copy(ref, ref, send_sem.at[s]).wait()

        for peer in line_peers:
            send(q_own, q_all.at[own_line], 0, peer)
        keep(q_own, q_all.at[own_line], 0)

        def landing_slot(slot):
            return steps.index((ring - steps[slot]) % ring)

        for slot in reversed(range(1, ring)):
            off, there = steps[slot], landing_slot(slot)

            @pl.when(z + off >= ring)
            def _(off=off, there=there):
                rows_there = pl.ds(pl.multiple_of(there * plane + y * 16, 16), 16)
                for k in reversed(range(lines)):
                    send(q_own, q_all.at[rows_there], 8 + there // 2, at(k, off))

        @pl.when(z < ring - 1)
        def _():
            for off in range(1, ring):
                @pl.when(z >= off)
                def _(off=off):
                    pl.semaphore_signal(
                        above.at[z + 1], inc=1, device_id=at(0, ring - off), device_id_type=MESH
                    )

        send(global_hbm, global_kv.at[:, own_span], 1, sibling)
        send(team_hbm, team_kv.at[core], 2, sibling)
        send(weight_hbm, weight.at[core], 3, sibling)

        for copy in small[1:]:
            copy.wait()

        agents = map_ref.shape[1]
        team_of = map_ref[...]
        agent = iota((1, agents), 1)
        mine = lax.rem(agent // 2, 2) == core
        before = (iota((agents, agents), 0) < iota((agents, agents), 1)).astype(BF16)
        row_agent = iota((agents, rows), 1)
        slot = row_agent // plane
        step = jnp.where(slot % 2 == 1, (slot + 1) // 2, ring - slot // 2)
        row_chip = (row_agent // 16) % lines * ring + (z + step) % ring
        row_agent = row_chip * 4 + core * 2 + (row_agent // 8) % 2
        spread = (iota((agents, rows), 0) == row_agent).astype(BF16)
        owner = owner_ref[...]
        team_ids = iota(owner.shape, 1)
        picks, hidden = [], []
        for slot in range(2):
            here = owner == chip * 2 + slot
            team = jnp.sum(jnp.where(here, team_ids, 0), axis=1, keepdims=True)
            length = jnp.sum(jnp.where(here, lengths_ref[...], 0), axis=1, keepdims=True)
            hidden.append(jnp.where(iota((1, team_hbm.shape[1]), 1) < length, 0.0, NEG))
            member = jnp.logical_and(team_of == team, mine)
            members = jnp.broadcast_to(jnp.where(member, 1.0, 0.0), (8, agents)).astype(BF16)
            rank = dot(members, before)[0:1]
            code = jnp.where(member, rank, 255.0)
            picks.append(dot(jnp.broadcast_to(code, (8, agents)).astype(BF16), spread)[0:1])
        place = iota((TEAM_CAP * 8, rows), 0)
        same_head = place % 8 == iota((TEAM_CAP * 8, rows), 1) % 8
        take = jnp.concatenate(
            [
                jnp.where(
                    jnp.logical_and(code == (place // 8).astype(F32), same_head), 1.0, 0.0
                )
                for code in picks
            ],
            axis=0,
        )
        give = take.T
        is_team = give > 0.5
        give = give.astype(BF16)
        take = take.astype(BF16)

        local[2].wait()
        suffix_num, suffix_lse = [], []
        for i in range(2):
            scores = dot_t(q_own[...], suffix_kv[0, i])[i * 8 : i * 8 + 8]
            seen = iota(scores.shape, 1) < suffix_len_ref[i]
            high = jnp.max(jnp.where(seen, scores, NEG), axis=-1, keepdims=True)
            weights = jnp.where(seen, jnp.exp((jnp.minimum(scores, high) - high) * scaling), 0.0)
            mass = jnp.sum(weights, axis=-1, keepdims=True)
            weights = jnp.concatenate([weights, weights], axis=0).astype(BF16)
            num = dot(weights, suffix_kv[1, i])[0:8]
            suffix_num.append(num / mass)
            suffix_lse.append(high * scaling + jnp.log(mass))
        suffix_num = jnp.concatenate(suffix_num, axis=0)
        suffix_lse = jnp.concatenate(suffix_lse, axis=0)
        others = rows // RING * 2 - plane
        suffix_num = jnp.concatenate([suffix_num] * lines + [jnp.zeros((others, 128), F32)], axis=0)
        suffix_lse = jnp.concatenate(
            [jnp.where(y == j, suffix_lse, NEG) for j in range(lines)]
            + [jnp.full((others, 1), NEG, F32)],
            axis=0,
        )

        own_plane = q_all.at[pl.ds(0, plane)]
        arrived(own_plane, 0)
        for off in range(1, ring):
            there = landing_slot(steps.index(off))

            @pl.when(z + off < ring)
            def _(off=off, there=there):
                if off > 1:
                    pl.semaphore_wait(above.at[z + off], 1)
                send(own_plane, q_all.at[pl.ds(there * plane, plane)], 8 + there // 2, at(0, off))

        chunk = 2 * plane
        chunks = rows // chunk
        local[0].wait()
        arrived(global_hbm, 1)
        prompt = []
        for c in range(chunks):
            first = c * chunk + (plane if c == 0 else 0)
            arrived(q_all.at[pl.ds(first, (c + 1) * chunk - first)], 8 + c)
            scores = dot_t(q_all[pl.ds(c * chunk, chunk), :], global_kv[0])
            num, high, mass = softmax_part(scores, global_kv[1], scaling)
            part = num * (1.0 / mass), high * scaling + jnp.log(mass)
            if c == 0:
                part = fold(part, (suffix_num, suffix_lse))
            prompt.append(part)

        @pl.when(z == 0)
        def _():
            for k in range(1, head_devices):
                pl.semaphore_signal(word.at[0], inc=1, device_id=head_peer(k, 0), device_id_type=MESH)

        local[1].wait()
        arrived(team_hbm, 2)
        team_rows = dot(take, q_all[...]).astype(BF16)
        team_num, team_lse = [], []
        for slot in range(2):
            block = TEAM_CAP * 8
            scores = dot_t(team_rows[slot * block : slot * block + block], team_kv[slot, 0])
            scores = scores + hidden[slot]
            num, high, mass = softmax_part(scores, team_kv[slot, 1], scaling)
            team_num.append(num * (1.0 / mass))
            team_lse.append(high * scaling + jnp.log(mass))
        team_num = jnp.concatenate(team_num, axis=0)
        team_lse = jnp.concatenate(team_lse, axis=0)
        eye = iota((128, 128), 0) == iota((128, 128), 1)
        lse_lane = jnp.max(jnp.where(eye, team_lse, NEG), axis=0, keepdims=True)
        coarse = team_num.astype(BF16)
        team_num = jnp.concatenate([coarse, (team_num - coarse.astype(F32)).astype(BF16)], axis=1)

        for c in range(chunks):
            span_rows = pl.ds(c * chunk, chunk)
            num = dot(give[c * chunk : c * chunk + chunk], team_num)
            lse = jnp.where(is_team[c * chunk : c * chunk + chunk], lse_lane, NEG)
            lse = jnp.max(lse, axis=-1, keepdims=True)
            num, lse = fold(prompt[c], (num[:, :128] + num[:, 128:], lse))
            part_out[span_rows, :] = num.astype(BF16)
            lse = jnp.where(
                iota((chunk, 128), 1) == iota((chunk, 128), 0) % 16, lse, 0.0
            )
            lse_out[pl.ds(c * chunk // 16, chunk // 16)] = jnp.sum(
                lse.reshape(chunk // 16, 16, 128), axis=1, keepdims=True
            )

        far_side = lax.rem(h, 2)

        def block_of(line, at_ring):
            middle = (line + 1) // 2 % 2
            row_line = line // 2 * 2 + at_ring // 4
            off = (at_ring % 4 + 4 * ((far_side + middle) % 2) - z + ring) % ring
            some, back = (off + ring - 1) // ring, (off + ring // 2 - 1) // ring
            slot = (1 - back) * (2 * off - some) + back * 2 * (ring - off)
            return slot * lines + row_line

        for slot in reversed(range(ring)):
            for k in reversed(range(lines)):
                if slot or k:
                    block = block_of(lax.rem(y + k, lines), lax.rem(z + steps[slot], ring))
                    peer = at(k, steps[slot])
                    send(part_out.at[pl.ds(pl.multiple_of(block * 16, 16), 16)], part_in.at[own_rows], 4, peer)
                    send(lse_out.at[block], lse_in.at[chip], 5, peer)
        block = block_of(y, z)
        keep(part_out.at[pl.ds(pl.multiple_of(block * 16, 16), 16)], part_in.at[own_rows], 4)
        keep(lse_out.at[block], lse_in.at[chip], 5)
        arrived(lse_in, 5)
        lse = lse_in[...].reshape(chips, 128)
        lse = jnp.concatenate([lse, jnp.full((128 - chips, 128), NEG, F32)], axis=0).T[0:16]
        factors = jnp.exp(lse - jnp.max(lse, axis=-1, keepdims=True))
        factors = factors / jnp.sum(factors, axis=-1, keepdims=True)
        arrived(part_in, 4)
        num = part_in[pl.ds(0, 16), :].astype(F32) * factors[:, 0:1]
        for j in range(1, chips):
            num = num + part_in[pl.ds(j * 16, 16), :].astype(F32) * factors[:, j : j + 1]
        att_own[...] = num.astype(BF16)

        kind = 12 + (y + 1) // 2 % 2
        for slot in reversed(range(ring)):
            for k in reversed(range(lines)):
                if slot or k:
                    send(att_own, att_all.at[own_rows], kind, at(k, steps[slot]))
        keep(att_own, att_all.at[own_rows], kind)

        @pl.when(z == 0)
        def _():
            pl.semaphore_wait(word.at[0], head_devices - 1)
            for peer in ring_peers:
                pl.semaphore_signal(word.at[1], inc=1, device_id=peer, device_id_type=MESH)

        local[3].wait()
        arrived(weight_hbm, 3)

        def project(spans, units):
            parts = []
            for start, size in spans:
                att_f32[pl.ds(start, size), :] = att_all[pl.ds(start, size), :].astype(F32)
            for j in range(8):
                parts.append(
                    jnp.concatenate(
                        [att_f32[pl.ds(start + j, size // 8, stride=8), :] for start, size in spans], axis=0
                    )
                )
            att = jnp.concatenate(parts, axis=1).astype(BF16)
            for side in range(2):
                sums = dot(att, weight[side]).astype(BF16).reshape(len(units), 8, 128)
                for n, unit in enumerate(units):
                    proj_out[side * head_devices + unit] = sums[n]

        def to_heads(side_of, unit_of):
            for d in (1, 0):
                to_core = lax.rem(core + d, 2)
                for k in (2, 1, 3, 0):
                    line = lax.rem(h // 2 + k, head_devices // 2)
                    there = line * 2 + side_of
                    src = proj_out.at[to_core * head_devices + unit_of(line)]
                    yield k, d, src, (chip * 2 + to_core, there)

        arrived(att_all.at[pl.ds(0, rows // 2)], 13)
        project([(rows // 4, rows // 2)], [2, 3, 4, 5])

        @pl.when(z != 0)
        def _():
            pl.semaphore_wait(word.at[1], 1)

        landing = proj_in.at[core * head_devices + h]
        for k, d, src, peer in to_heads(1 - far_side, lambda line: 2 + line):
            send(src, landing, 7, peer)
        arrived(att_all.at[pl.ds(0, rows // 2)], 12)
        project([(0, rows // 4), (3 * rows // 4, rows // 4)], [0, 1, 6, 7])
        for k, d, src, peer in to_heads(far_side, lambda line: line // 2 * 6 + line % 2):
            if k or d:
                send(src, landing, 7, peer)
            else:
                keep(src, landing, 7)
        arrived(proj_in, 7)
        for side in range(2):
            summed = jnp.sum(proj_in[pl.ds(side * head_devices, head_devices)].astype(F32), axis=0)
            for j in range(4):
                merged[pl.ds(4 * j + 2 * side, 2), :] = summed[2 * j : 2 * j + 2]
        out_ref[...] = merged[...].astype(BF16)

        others = pl.ds(0, (chips - 1) * 16)
        sent(q_all.at[pl.ds(0, plane - 16)], 0)
        for c in range(chunks):
            first = c * chunk + (plane if c == 0 else 0)
            sent(q_all.at[pl.ds(first, (c + 1) * chunk - first)], 8 + c)
        sent(global_hbm, 1)
        sent(team_hbm, 2)
        sent(weight_hbm, 3)
        sent(part_in.at[others], 4)
        sent(lse_in.at[pl.ds(0, chips - 1)], 5)
        sent(att_all.at[others], kind)
        sent(proj_in.at[pl.ds(0, len(heads))], 7)

    return kernel, rows, chips


def shards(queries, global_kv, team_kv, suffix_kv, team_lengths, team_map, suffix_lengths, team_owner, out_weight):
    agent_devices = lax.axis_size("agents")
    head_devices = lax.axis_size("heads")
    kernel, rows, chips = make_kernel(agent_devices, head_devices)
    vmem = pl.BlockSpec(memory_space=pltpu.VMEM)
    hbm = pl.BlockSpec(memory_space=pltpu.HBM)
    span = global_kv.shape[1]
    out_rows = rows * 2 // 8 // head_devices
    return pl.pallas_call(
        kernel,
        out_shape=pltpu.VMEM((out_rows, out_weight.shape[1]), BF16),
        in_specs=[hbm] * 9,
        out_specs=vmem,
        scratch_shapes=[
            pltpu.VMEM(queries.shape, BF16),
            pltpu.VMEM((1,) + team_lengths.shape, jnp.int32),
            pltpu.VMEM((1,) + team_map.shape, jnp.int32),
            pltpu.VMEM((1,) + team_owner.shape, jnp.int32),
            pltpu.SMEM(suffix_lengths.shape, jnp.int32),
            pltpu.VMEM((16, 128), F32),
            pltpu.VMEM((16, 128), BF16),
            pltpu.VMEM((rows, 128), BF16),
            pltpu.VMEM((2, 2 * span, 128), BF16),
            pltpu.VMEM((2,) + team_kv.shape, BF16),
            pltpu.VMEM(suffix_kv.shape, BF16),
            pltpu.VMEM((2,) + out_weight.shape, BF16),
            pltpu.VMEM((rows, 128), BF16),
            pltpu.VMEM((rows, 128), BF16),
            pltpu.VMEM((chips, 1, 128), F32),
            pltpu.VMEM((chips, 1, 128), F32),
            pltpu.VMEM((16, 128), BF16),
            pltpu.VMEM((rows, 128), BF16),
            pltpu.VMEM((rows, 128), F32),
            pltpu.VMEM((2 * head_devices, 8, 128), BF16),
            pltpu.VMEM((2 * head_devices, 8, 128), BF16),
            pltpu.VMEM((16, 128), F32),
            pltpu.SemaphoreType.DMA((9,)),
            pltpu.SemaphoreType.DMA((14,)),
            pltpu.SemaphoreType.DMA((14,)),
            pltpu.SemaphoreType.REGULAR((2,)),
            pltpu.SemaphoreType.REGULAR((RING,)),
        ],
        compiler_params=pltpu.CompilerParams(
            collective_id=0, has_side_effects=True, vmem_limit_bytes=62 * 1024 * 1024
        ),
        name="decode",
    )(
        queries,
        team_lengths.reshape(1, -1),
        team_map.reshape(1, -1),
        team_owner.reshape(1, -1),
        suffix_lengths,
        global_kv,
        team_kv,
        suffix_kv,
        out_weight,
    )


def solution(mesh):
    return jax.shard_map(
        shards,
        mesh=mesh,
        in_specs=(
            P("agents", "heads"),
            P(None, "agents", "heads"),
            P(None, "agents", "heads"),
            P(None, "agents", None, "heads"),
            P(),
            P(),
            P("agents"),
            P(),
            P("heads", "agents"),
        ),
        out_specs=P("heads", "agents"),
        check_vma=False,
    )
```

```python
import math

import jax
import jax.numpy as jnp
from jax import lax
from jax.experimental import pallas as pl
from jax.experimental.pallas import tpu as pltpu
from jax.sharding import PartitionSpec as P

HEAD_DIM = 128
TEAM_CAP = 8
RING = 8
NEG = -1e30
LOG2E = math.log2(math.e)
MESH = pl.DeviceIdType.MESH
F32 = jnp.float32
BF16 = jnp.bfloat16


def dot(a, b):
    return jnp.dot(a, b, preferred_element_type=F32)


def dot_t(a, b):
    return lax.dot_general(a, b, (((1,), (1,)), ((), ())), preferred_element_type=F32)


def iota(shape, dim):
    return lax.broadcasted_iota(jnp.int32, shape, dim)


def softmax_part(scores, values, scaling):
    high = jnp.max(scores, axis=-1, keepdims=True)
    weights = jnp.exp2((scores - high) * (scaling * LOG2E))
    mass = jnp.sum(weights, axis=-1, keepdims=True)
    return dot(weights.astype(BF16), values), high, mass


def fold(first, second):
    top = jnp.maximum(first[1], second[1])
    one, two = jnp.exp(first[1] - top), jnp.exp(second[1] - top)
    total = one + two
    return first[0] * (one / total) + second[0] * (two / total), top + jnp.log(total)


def make_kernel(agent_devices, head_devices):
    chips = agent_devices // 2
    rows = chips * 16

    def kernel(
        q_hbm, lengths_hbm, map_hbm, owner_hbm, suffix_len_hbm,
        global_hbm, team_hbm, suffix_hbm, weight_hbm,
        out_ref,
        q_ref, lengths_ref, map_ref, owner_ref, suffix_len_ref, q_f32, q_own, q_all, global_kv, team_kv, suffix_kv, weight,
        part_out, part_in, lse_out, lse_in, att_own, att_all, att_f32,
        proj_out, proj_in, merged,
        local_sem, send_sem, recv_sem, word, above,
    ):
        a = lax.axis_index("agents")
        h = lax.axis_index("heads")
        core = lax.rem(a, 2)
        chip = a // 2
        ring = RING
        lines = chips // ring
        z = lax.rem(chip, ring)
        y = chip // ring
        plane = lines * 16
        scaling = 1.0 / math.sqrt(HEAD_DIM)
        steps = [(s + 1) // 2 if s % 2 else (ring - s // 2) % ring for s in range(ring)]

        def at(dy, dz):
            return ((lax.rem(y + dy, lines) * ring + lax.rem(z + dz, ring)) * 2 + core, h)

        def head_peer(k, d):
            return (chip * 2 + lax.rem(core + d, 2), lax.rem(h + k, head_devices))

        sibling = head_peer(0, 1)
        line_peers = [at(k, 0) for k in range(1, lines)]
        ring_peers = [at(0, k) for k in range(1, ring)]
        heads = [(k, d) for k in range(head_devices) for d in range(2) if k or d]

        barrier = pltpu.get_barrier_semaphore()

        def hello(peer):
            pl.semaphore_signal(barrier, inc=1, device_id=peer, device_id_type=MESH)

        for peer in line_peers + [sibling]:
            hello(peer)

        @pl.when(z > 0)
        def _():
            hello(at(0, ring - 1))

        for off in range(1, ring):
            @pl.when(z + off < ring)
            def _(off=off):
                for k in range(lines):
                    hello(at(k, off))

        @pl.when(z == 0)
        def _():
            for k in range(1, head_devices):
                hello(head_peer(k, 0))

        span = global_hbm.shape[1]
        own_span = pl.ds(pl.multiple_of(core * span, span), span)
        small = [
            pltpu.make_async_copy(q_hbm, q_ref, local_sem.at[4]),
            pltpu.make_async_copy(lengths_hbm, lengths_ref, local_sem.at[5]),
            pltpu.make_async_copy(map_hbm, map_ref, local_sem.at[6]),
            pltpu.make_async_copy(owner_hbm, owner_ref, local_sem.at[7]),
            pltpu.make_async_copy(suffix_len_hbm, suffix_len_ref, local_sem.at[8]),
        ]
        local = [
            pltpu.make_async_copy(global_hbm, global_kv.at[:, own_span], local_sem.at[0]),
            pltpu.make_async_copy(team_hbm, team_kv.at[core], local_sem.at[1]),
            pltpu.make_async_copy(suffix_hbm, suffix_kv, local_sem.at[2]),
            pltpu.make_async_copy(weight_hbm, weight.at[core], local_sem.at[3]),
        ]
        for copy in small + local:
            copy.start()

        small[0].wait()
        for i in range(2):
            for j in range(8):
                q_f32[pl.ds(i * 8 + j, 1), :] = q_ref[
                    pl.ds(i, 1), pl.ds(j * HEAD_DIM, HEAD_DIM)
                ].astype(F32)
        q_own[...] = q_f32[...].astype(BF16)

        top_plane = (z + 1) // ring
        bottom_plane = 1 - (z + ring - 1) // ring
        pl.semaphore_wait(
            barrier, lines * (z + 1) + 1 - top_plane + (head_devices - 1) * bottom_plane
        )

        own_rows = pl.ds(pl.multiple_of(chip * 16, 16), 16)
        own_line = pl.ds(pl.multiple_of(y * 16, 16), 16)

        def send(src, dst, s, peer):
            copy = pltpu.make_async_remote_copy(
                src_ref=src, dst_ref=dst, send_sem=send_sem.at[s], recv_sem=recv_sem.at[s],
                device_id=peer, device_id_type=MESH,
            )
            copy.start()

        def keep(src, dst, s):
            pltpu.make_async_copy(src, dst, recv_sem.at[s]).start()

        def arrived(ref, s):
            pltpu.make_async_copy(ref, ref, recv_sem.at[s]).wait()

        def sent(ref, s):
            pltpu.make_async_copy(ref, ref, send_sem.at[s]).wait()

        for peer in line_peers:
            send(q_own, q_all.at[own_line], 0, peer)
        keep(q_own, q_all.at[own_line], 0)

        def landing_slot(slot):
            return steps.index((ring - steps[slot]) % ring)

        for slot in reversed(range(1, ring)):
            off, there = steps[slot], landing_slot(slot)

            @pl.when(z + off >= ring)
            def _(off=off, there=there):
                rows_there = pl.ds(pl.multiple_of(there * plane + y * 16, 16), 16)
                for k in reversed(range(lines)):
                    send(q_own, q_all.at[rows_there], 8 + there // 2, at(k, off))

        @pl.when(z < ring - 1)
        def _():
            for off in range(1, ring):
                @pl.when(z >= off)
                def _(off=off):
                    pl.semaphore_signal(
                        above.at[z + 1], inc=1, device_id=at(0, ring - off), device_id_type=MESH
                    )

        send(global_hbm, global_kv.at[:, own_span], 1, sibling)
        send(team_hbm, team_kv.at[core], 2, sibling)
        send(weight_hbm, weight.at[core], 3, sibling)

        for copy in small[1:]:
            copy.wait()

        agents = map_ref.shape[1]
        team_of = map_ref[...]
        agent = iota((1, agents), 1)
        mine = lax.rem(agent // 2, 2) == core
        before = (iota((agents, agents), 0) < iota((agents, agents), 1)).astype(BF16)
        row_agent = iota((agents, rows), 1)
        slot = row_agent // plane
        step = jnp.where(slot % 2 == 1, (slot + 1) // 2, ring - slot // 2)
        row_chip = (row_agent // 16) % lines * ring + (z + step) % ring
        row_agent = row_chip * 4 + core * 2 + (row_agent // 8) % 2
        spread = (iota((agents, rows), 0) == row_agent).astype(BF16)
        owner = owner_ref[...]
        team_ids = iota(owner.shape, 1)
        picks, hidden = [], []
        for slot in range(2):
            here = owner == chip * 2 + slot
            team = jnp.sum(jnp.where(here, team_ids, 0), axis=1, keepdims=True)
            length = jnp.sum(jnp.where(here, lengths_ref[...], 0), axis=1, keepdims=True)
            hidden.append(jnp.where(iota((1, team_hbm.shape[1]), 1) < length, 0.0, NEG))
            member = jnp.logical_and(team_of == team, mine)
            members = jnp.broadcast_to(jnp.where(member, 1.0, 0.0), (8, agents)).astype(BF16)
            rank = dot(members, before)[0:1]
            code = jnp.where(member, rank, 255.0)
            picks.append(dot(jnp.broadcast_to(code, (8, agents)).astype(BF16), spread)[0:1])
        place = iota((TEAM_CAP * 8, rows), 0)
        same_head = place % 8 == iota((TEAM_CAP * 8, rows), 1) % 8
        take = jnp.concatenate(
            [
                jnp.where(
                    jnp.logical_and(code == (place // 8).astype(F32), same_head), 1.0, 0.0
                )
                for code in picks
            ],
            axis=0,
        )
        give = take.T
        is_team = give > 0.5
        give = give.astype(BF16)
        take = take.astype(BF16)

        local[2].wait()
        suffix_num, suffix_lse = [], []
        for i in range(2):
            scores = dot_t(q_own[...], suffix_kv[0, i])[i * 8 : i * 8 + 8]
            seen = iota(scores.shape, 1) < suffix_len_ref[i]
            high = jnp.max(jnp.where(seen, scores, NEG), axis=-1, keepdims=True)
            weights = jnp.where(seen, jnp.exp((jnp.minimum(scores, high) - high) * scaling), 0.0)
            mass = jnp.sum(weights, axis=-1, keepdims=True)
            weights = jnp.concatenate([weights, weights], axis=0).astype(BF16)
            num = dot(weights, suffix_kv[1, i])[0:8]
            suffix_num.append(num / mass)
            suffix_lse.append(high * scaling + jnp.log(mass))
        suffix_num = jnp.concatenate(suffix_num, axis=0)
        suffix_lse = jnp.concatenate(suffix_lse, axis=0)
        others = rows // RING * 2 - plane
        suffix_num = jnp.concatenate([suffix_num] * lines + [jnp.zeros((others, 128), F32)], axis=0)
        suffix_lse = jnp.concatenate(
            [jnp.where(y == j, suffix_lse, NEG) for j in range(lines)]
            + [jnp.full((others, 1), NEG, F32)],
            axis=0,
        )

        own_plane = q_all.at[pl.ds(0, plane)]
        arrived(own_plane, 0)
        for off in range(1, ring):
            there = landing_slot(steps.index(off))

            @pl.when(z + off < ring)
            def _(off=off, there=there):
                if off > 1:
                    pl.semaphore_wait(above.at[z + off], 1)
                send(own_plane, q_all.at[pl.ds(there * plane, plane)], 8 + there // 2, at(0, off))

        chunk = 2 * plane
        chunks = rows // chunk
        local[0].wait()
        arrived(global_hbm, 1)
        prompt = []
        for c in range(chunks):
            first = c * chunk + (plane if c == 0 else 0)
            arrived(q_all.at[pl.ds(first, (c + 1) * chunk - first)], 8 + c)
            scores = dot_t(q_all[pl.ds(c * chunk, chunk), :], global_kv[0])
            num, high, mass = softmax_part(scores, global_kv[1], scaling)
            part = num * (1.0 / mass), high * scaling + jnp.log(mass)
            if c == 0:
                part = fold(part, (suffix_num, suffix_lse))
            prompt.append(part)

        @pl.when(z == 0)
        def _():
            for k in range(1, head_devices):
                pl.semaphore_signal(word.at[0], inc=1, device_id=head_peer(k, 0), device_id_type=MESH)

        local[1].wait()
        arrived(team_hbm, 2)
        team_rows = dot(take, q_all[...]).astype(BF16)
        team_num, team_lse = [], []
        for slot in range(2):
            block = TEAM_CAP * 8
            scores = dot_t(team_rows[slot * block : slot * block + block], team_kv[slot, 0])
            scores = scores + hidden[slot]
            num, high, mass = softmax_part(scores, team_kv[slot, 1], scaling)
            team_num.append(num * (1.0 / mass))
            team_lse.append(high * scaling + jnp.log(mass))
        team_num = jnp.concatenate(team_num, axis=0)
        team_lse = jnp.concatenate(team_lse, axis=0)
        eye = iota((128, 128), 0) == iota((128, 128), 1)
        lse_lane = jnp.max(jnp.where(eye, team_lse, NEG), axis=0, keepdims=True)
        coarse = team_num.astype(BF16)
        team_num = jnp.concatenate([coarse, (team_num - coarse.astype(F32)).astype(BF16)], axis=1)

        for c in range(chunks):
            span_rows = pl.ds(c * chunk, chunk)
            num = dot(give[c * chunk : c * chunk + chunk], team_num)
            lse = jnp.where(is_team[c * chunk : c * chunk + chunk], lse_lane, NEG)
            lse = jnp.max(lse, axis=-1, keepdims=True)
            num, lse = fold(prompt[c], (num[:, :128] + num[:, 128:], lse))
            part_out[span_rows, :] = num.astype(BF16)
            lse = jnp.where(
                iota((chunk, 128), 1) == iota((chunk, 128), 0) % 16, lse, 0.0
            )
            lse_out[pl.ds(c * chunk // 16, chunk // 16)] = jnp.sum(
                lse.reshape(chunk // 16, 16, 128), axis=1, keepdims=True
            )

        far_side = lax.rem(h, 2)
        upper = y // 2
        hops = [min(step, ring - step) for step in steps]
        order = sorted(((s, t) for s in range(ring) for t in range(lines)), key=lambda p: p[1] - hops[p[0]])

        def line_of(slot, t):
            if slot == 0:
                return lax.rem(y + lines - 1 - t, lines)
            return (1 - upper) * (lines - 1 - t) + upper * t

        def block_of(line, at_ring):
            middle = (line + 1) // 2 % 2
            row_line = line // 2 * 2 + at_ring // 4
            off = (at_ring % 4 + 4 * ((far_side + middle) % 2) - z + ring) % ring
            some, back = (off + ring - 1) // ring, (off + ring // 2 - 1) // ring
            slot = (1 - back) * (2 * off - some) + back * 2 * (ring - off)
            return slot * lines + row_line

        for slot, t in order:
                if slot or t < lines - 1:
                    to_line = line_of(slot, t)
                    block = block_of(to_line, lax.rem(z + steps[slot], ring))
                    peer = at(to_line - y + lines, steps[slot])
                    send(part_out.at[pl.ds(pl.multiple_of(block * 16, 16), 16)], part_in.at[own_rows], 4, peer)
                    send(lse_out.at[block], lse_in.at[chip], 5, peer)
        block = block_of(y, z)
        keep(part_out.at[pl.ds(pl.multiple_of(block * 16, 16), 16)], part_in.at[own_rows], 4)
        keep(lse_out.at[block], lse_in.at[chip], 5)
        arrived(lse_in, 5)
        lse = lse_in[...].reshape(chips, 128)
        lse = jnp.concatenate([lse, jnp.full((128 - chips, 128), NEG, F32)], axis=0).T[0:16]
        factors = jnp.exp(lse - jnp.max(lse, axis=-1, keepdims=True))
        factors = factors / jnp.sum(factors, axis=-1, keepdims=True)
        arrived(part_in, 4)
        num = part_in[pl.ds(0, 16), :].astype(F32) * factors[:, 0:1]
        for j in range(1, chips):
            num = num + part_in[pl.ds(j * 16, 16), :].astype(F32) * factors[:, j : j + 1]
        att_own[...] = num.astype(BF16)

        kind = 12 + (y + 1) // 2 % 2
        for slot, t in order:
            if slot or t < lines - 1:
                send(att_own, att_all.at[own_rows], kind, at(line_of(slot, t) - y + lines, steps[slot]))
        keep(att_own, att_all.at[own_rows], kind)

        @pl.when(z == 0)
        def _():
            pl.semaphore_wait(word.at[0], head_devices - 1)
            for peer in ring_peers:
                pl.semaphore_signal(word.at[1], inc=1, device_id=peer, device_id_type=MESH)

        local[3].wait()
        arrived(weight_hbm, 3)

        def project(spans, units):
            parts = []
            for start, size in spans:
                att_f32[pl.ds(start, size), :] = att_all[pl.ds(start, size), :].astype(F32)
            for j in range(8):
                parts.append(
                    jnp.concatenate(
                        [att_f32[pl.ds(start + j, size // 8, stride=8), :] for start, size in spans], axis=0
                    )
                )
            att = jnp.concatenate(parts, axis=1).astype(BF16)
            for side in range(2):
                sums = dot(att, weight[side]).astype(BF16).reshape(len(units), 8, 128)
                for n, unit in enumerate(units):
                    proj_out[side * head_devices + unit] = sums[n]

        def to_heads(side_of, unit_of):
            for d in (1, 0):
                to_core = lax.rem(core + d, 2)
                for k in (2, 1, 3, 0):
                    line = lax.rem(h // 2 + k, head_devices // 2)
                    there = line * 2 + side_of
                    src = proj_out.at[to_core * head_devices + unit_of(line)]
                    yield k, d, src, (chip * 2 + to_core, there)

        arrived(att_all.at[pl.ds(0, rows // 2)], 13)
        project([(rows // 4, rows // 2)], [2, 3, 4, 5])

        @pl.when(z != 0)
        def _():
            pl.semaphore_wait(word.at[1], 1)

        landing = proj_in.at[core * head_devices + h]
        for k, d, src, peer in to_heads(1 - far_side, lambda line: 2 + line):
            send(src, landing, 7, peer)
        arrived(att_all.at[pl.ds(0, rows // 2)], 12)
        project([(0, rows // 4), (3 * rows // 4, rows // 4)], [0, 1, 6, 7])
        for k, d, src, peer in to_heads(far_side, lambda line: line // 2 * 6 + line % 2):
            if k or d:
                send(src, landing, 7, peer)
            else:
                keep(src, landing, 7)
        arrived(proj_in, 7)
        for side in range(2):
            summed = jnp.sum(proj_in[pl.ds(side * head_devices, head_devices)].astype(F32), axis=0)
            for j in range(4):
                merged[pl.ds(4 * j + 2 * side, 2), :] = summed[2 * j : 2 * j + 2]
        out_ref[...] = merged[...].astype(BF16)

        others = pl.ds(0, (chips - 1) * 16)
        sent(q_all.at[pl.ds(0, plane - 16)], 0)
        for c in range(chunks):
            first = c * chunk + (plane if c == 0 else 0)
            sent(q_all.at[pl.ds(first, (c + 1) * chunk - first)], 8 + c)
        sent(global_hbm, 1)
        sent(team_hbm, 2)
        sent(weight_hbm, 3)
        sent(part_in.at[others], 4)
        sent(lse_in.at[pl.ds(0, chips - 1)], 5)
        sent(att_all.at[others], kind)
        sent(proj_in.at[pl.ds(0, len(heads))], 7)

    return kernel, rows, chips


def shards(queries, global_kv, team_kv, suffix_kv, team_lengths, team_map, suffix_lengths, team_owner, out_weight):
    agent_devices = lax.axis_size("agents")
    head_devices = lax.axis_size("heads")
    kernel, rows, chips = make_kernel(agent_devices, head_devices)
    vmem = pl.BlockSpec(memory_space=pltpu.VMEM)
    hbm = pl.BlockSpec(memory_space=pltpu.HBM)
    span = global_kv.shape[1]
    out_rows = rows * 2 // 8 // head_devices
    return pl.pallas_call(
        kernel,
        out_shape=pltpu.VMEM((out_rows, out_weight.shape[1]), BF16),
        in_specs=[hbm] * 9,
        out_specs=vmem,
        scratch_shapes=[
            pltpu.VMEM(queries.shape, BF16),
            pltpu.VMEM((1,) + team_lengths.shape, jnp.int32),
            pltpu.VMEM((1,) + team_map.shape, jnp.int32),
            pltpu.VMEM((1,) + team_owner.shape, jnp.int32),
            pltpu.SMEM(suffix_lengths.shape, jnp.int32),
            pltpu.VMEM((16, 128), F32),
            pltpu.VMEM((16, 128), BF16),
            pltpu.VMEM((rows, 128), BF16),
            pltpu.VMEM((2, 2 * span, 128), BF16),
            pltpu.VMEM((2,) + team_kv.shape, BF16),
            pltpu.VMEM(suffix_kv.shape, BF16),
            pltpu.VMEM((2,) + out_weight.shape, BF16),
            pltpu.VMEM((rows, 128), BF16),
            pltpu.VMEM((rows, 128), BF16),
            pltpu.VMEM((chips, 1, 128), F32),
            pltpu.VMEM((chips, 1, 128), F32),
            pltpu.VMEM((16, 128), BF16),
            pltpu.VMEM((rows, 128), BF16),
            pltpu.VMEM((rows, 128), F32),
            pltpu.VMEM((2 * head_devices, 8, 128), BF16),
            pltpu.VMEM((2 * head_devices, 8, 128), BF16),
            pltpu.VMEM((16, 128), F32),
            pltpu.SemaphoreType.DMA((9,)),
            pltpu.SemaphoreType.DMA((14,)),
            pltpu.SemaphoreType.DMA((14,)),
            pltpu.SemaphoreType.REGULAR((2,)),
            pltpu.SemaphoreType.REGULAR((RING,)),
        ],
        compiler_params=pltpu.CompilerParams(
            collective_id=0, has_side_effects=True, vmem_limit_bytes=62 * 1024 * 1024
        ),
        name="decode",
    )(
        queries,
        team_lengths.reshape(1, -1),
        team_map.reshape(1, -1),
        team_owner.reshape(1, -1),
        suffix_lengths,
        global_kv,
        team_kv,
        suffix_kv,
        out_weight,
    )


def solution(mesh):
    return jax.shard_map(
        shards,
        mesh=mesh,
        in_specs=(
            P("agents", "heads"),
            P(None, "agents", "heads"),
            P(None, "agents", "heads"),
            P(None, "agents", None, "heads"),
            P(),
            P(),
            P("agents"),
            P(),
            P("heads", "agents"),
        ),
        out_specs=P("heads", "agents"),
        check_vma=False,
    )
```
